256 devices in a mesh: row: 16 (over z_hi, y, core), col: 16 (over x, z_lo).
Axes of the slice: x: 4, y: 4, z: 8 (z_hi: 2, z_lo: 4; z = z_hi * 4 + z_lo), core: 2. Of those that a mesh axis runs over, the one named last changes fastest.
Arguments:
- slab_points: bfloat16 [64, 16384], P(None, ('row', 'col')), may hold values from -6 to 6
- col_points: bfloat16 [64, 262144], P(None, 'col'), may hold values from -6 to 6
- probes: bfloat16 [64, 262144], P(None, 'col'), may hold values from -6 to 6
Outputs:
- basis: bfloat16 [64, 16384], P(None, ('row', 'col'))
- image: float32 [64, 262144], P(None, ('col', 'row'))
The draws below stay inside these ranges and needn't reach their ends.
All inputs are finite; a program needn't handle non-finite values.
Results may differ from the reference program's by a relative error of at most 0.0052.
Values may be sent and summed in bfloat16 or wider, within the bound.
A program may use at most 128 MiB of HBM per device.

```python
import math
import jax
import jax.numpy as jnp
from jax import lax

DIM = 64
PROBES = 64
SLAB = 16384
NPTS = 262144


def draw_slab_points(key, part):
    key = jax.random.fold_in(key, 17)
    values = jnp.clip(jax.random.normal(key, (DIM, SLAB), jnp.float32), -6.0, 6.0)
    return values.astype(jnp.bfloat16)


def draw_col_points(key, part):
    key = jax.random.fold_in(key, 29)
    values = jnp.clip(jax.random.normal(key, (DIM, NPTS), jnp.float32), -6.0, 6.0)
    return values.astype(jnp.bfloat16)


def levels(key, extent, cuts, least, top_value):
    def one(position, blocks):
        draws = jax.random.uniform(jax.random.fold_in(jax.random.fold_in(key, 6), position), (blocks,), jnp.float32, least / len(cuts), top_value / len(cuts))
        return jnp.repeat(jnp.exp(draws), extent[position] // blocks).reshape((-1,) + (1,) * (len(extent) - position - 1))

    level = one(*cuts[0])
    for cut in cuts[1:]:
        level = level * one(*cut)
    return level


def bell_draw(rng, shape, scale, limit, shards=(), kind=jnp.bfloat16):
    loudness = levels(rng, shape, shards, -0.22, 0.18) if shards else 1.0
    entries = jax.random.normal(rng, shape, jnp.float32) * scale * loudness
    return jnp.minimum(jnp.maximum(entries, -limit), limit).astype(kind)


def setup_inputs(seed: int = 0) -> dict:
    seeds = jax.random.split(jax.random.key(seed), 4)
    return {
        "slab_points": draw_slab_points(jax.random.fold_in(seeds[3], 71), 0),
        "col_points": draw_col_points(jax.random.fold_in(seeds[3], 71), 0),
        "probes": bell_draw(seeds[2], (PROBES, NPTS), 1.0, 6.0, ((1, 16),)),
    }


def kernel_block(slab_points, slab_norm, col_block, norm_block):
    inner = lax.dot_general(slab_points.astype(jnp.float32), col_block.astype(jnp.float32), (((0,), (0,)), ((), ())), preferred_element_type=jnp.float32)
    distance = slab_norm[:, None] + norm_block[None, :] - 2.0 * inner
    return jnp.exp(-8.0 * distance / DIM).astype(jnp.bfloat16)

def reference(slab_points, col_points, probes):
    slab_norm = lax.optimization_barrier(jnp.sum(slab_points.astype(jnp.float32) ** 2, axis=0))
    col_norm = lax.optimization_barrier(jnp.sum(col_points.astype(jnp.float32) ** 2, axis=0))
    width = math.gcd(NPTS, 4096)
    count = NPTS // width

    def sample_step(total, which):
        start = (which * width).astype(jnp.int32)
        cols = lax.dynamic_slice_in_dim(col_points, start, width, 1)
        norms = lax.dynamic_slice_in_dim(col_norm, start, width, 0)
        kernel = kernel_block(slab_points, slab_norm, cols, norms)
        probe_block = lax.dynamic_slice_in_dim(probes, start, width, 1)
        return (total + lax.dot_general(probe_block.astype(jnp.float32), kernel.astype(jnp.float32), (((1,), (1,)), ((), ())), preferred_element_type=jnp.float32), None)
    sample, unused = lax.scan(sample_step, jnp.zeros((PROBES, SLAB), jnp.float32), jnp.arange(count, dtype=jnp.int32))
    gram = jnp.dot(sample, sample.T, precision=lax.Precision.HIGHEST) / SLAB
    lower = jnp.linalg.cholesky(gram)
    basis = jax.scipy.linalg.solve_triangular(lower, sample, lower=True).astype(jnp.bfloat16)

    def image_step(carry, which):
        start = (which * width).astype(jnp.int32)
        cols = lax.dynamic_slice_in_dim(col_points, start, width, 1)
        norms = lax.dynamic_slice_in_dim(col_norm, start, width, 0)
        kernel = kernel_block(slab_points, slab_norm, cols, norms)
        return (carry, jnp.dot(basis.astype(jnp.float32), kernel.astype(jnp.float32), preferred_element_type=jnp.float32))
    unused_carry, blocks = lax.scan(image_step, jnp.float32(0.0), jnp.arange(count, dtype=jnp.int32))
    image_scale = jnp.sqrt(jnp.float32(PROBES * NPTS) / jnp.trace(gram)) / SLAB
    image = jnp.transpose(blocks, (1, 0, 2)).reshape(PROBES, NPTS) * image_scale
    return (basis, image)
```

```python
import functools
import math

import jax
import jax.numpy as jnp
from jax import lax
from jax.experimental import pallas as pl
from jax.experimental.pallas import tpu as pltpu
from jax.sharding import PartitionSpec as P

F32 = jnp.float32
BF16 = jnp.bfloat16
MESH = pl.DeviceIdType.MESH
NN = (((1,), (0,)), ((), ()))
NT = (((1,), (1,)), ((), ()))
LOG2E = 1.4426950408889634
HIGHEST = lax.Precision.HIGHEST

NX, NZ, NY, NCORE = 4, 8, 4, 2
GROUP = NX * NZ
PEERS = NY * NCORE
DIMS = 64
PROBES = 64
BLK = 64
CHUNKS = 4
CA = 512
A = CHUNKS * CA
B = 8192
TB = 4096
OWN = 1024


def split3(v):
    h = v.astype(BF16).astype(F32)
    m = (v - h).astype(BF16).astype(F32)
    return h, m, v - h - m


def main_kernel(
    slab_ref, col_ref, probe_ref,
    zsum_ref, gsum_ref, sown_ref,
    cols, probes, yt, xall, xaug, kmat, spart, rsrecv, sfull, st,
    zsend, zmine, zcrecv, zyrecv, gsend, grecv, xown,
    in_sem, xs_sem, xr_sem, rs_s, rs_r, ag_s, ag_r, zc_s, zc_r, zy_s, zy_r, g_s, g_r,
):
    row = lax.axis_index("row")
    col = lax.axis_index("col")
    core = row % 2
    y = (row // 2) % 4
    z = (row // 8) * 4 + col % 4
    x = col // 4
    zhi = row // 8
    me = z * NX + x
    mine = y * NCORE + core
    my_chunk = (x - z + 8) % 4

    def group_id(g):
        gx = g % NX
        gz = g // NX
        return ((gz // 4) * 8 + y * 2 + core, gx * 4 + gz % 4)

    def peer_id(q):
        return (zhi * 8 + q, col)

    def owner(c, j):
        return j * NX + (c + j) % NX

    cp_c = pltpu.make_async_copy(col_ref.at[:, pl.ds(pl.multiple_of(zhi * B, B), B)], cols, in_sem.at[0])
    cp_p = pltpu.make_async_copy(
        probe_ref.at[:, pl.ds(pl.multiple_of(zhi * B, B), B)], probes.at[pl.ds(0, PROBES), :], in_sem.at[1]
    )
    cp_c.start()
    cp_p.start()

    barrier = pltpu.get_barrier_semaphore()

    def greet_group(r, _):
        pl.semaphore_signal(barrier, inc=1, device_id=group_id((me + r) % GROUP), device_id_type=MESH)
        return 0

    def greet_peer(r, _):
        pl.semaphore_signal(barrier, inc=1, device_id=peer_id((mine + r) % PEERS), device_id_type=MESH)
        return 0

    lax.fori_loop(1, GROUP, greet_group, 0)
    lax.fori_loop(1, PEERS, greet_peer, 0)

    s_in = slab_ref[...].astype(F32)
    packed = jnp.concatenate([s_in[: DIMS // 2], s_in[DIMS // 2 :]], axis=1).astype(BF16)
    xown[...] = packed
    xall[me] = packed
    probes[PROBES:, :] = jnp.zeros((128 - PROBES, B), BF16)

    pl.semaphore_wait(barrier, GROUP - 1 + PEERS - 1)

    def slab_copy(r):
        return pltpu.make_async_remote_copy(
            src_ref=xown,
            dst_ref=xall.at[me],
            send_sem=xs_sem.at[r - 1],
            recv_sem=xr_sem.at[me],
            device_id=group_id((me + r) % GROUP),
            device_id_type=MESH,
        )

    def slab_send(r, _):
        slab_copy(r).start()
        return 0

    lax.fori_loop(1, GROUP, slab_send, 0)

    cp_c.wait()
    alpha = LOG2E * 8.0 / DIMS

    def make_yt(i, _):
        b0 = pl.multiple_of(i * 512, 512)
        yv = cols[:, pl.ds(b0, 512)].astype(F32)
        yp = yv * (2.0 * alpha)
        h, m, l = split3(yp)
        nh, nm, nl = split3(-alpha * jnp.sum(yv * yv, axis=0, keepdims=True))
        r = lax.broadcasted_iota(jnp.int32, (DIMS, 512), 0)
        extra = jnp.where(
            r < 3, 1.0, jnp.where(r == 3, nh, jnp.where(r == 4, nm, jnp.where(r == 5, nl, 0.0)))
        )
        yt[pl.ds(b0, 512), 0:128] = jnp.transpose(jnp.concatenate([h, m], axis=0)).astype(BF16)
        yt[pl.ds(b0, 512), 128:256] = jnp.transpose(jnp.concatenate([l, extra], axis=0)).astype(BF16)
        return 0

    lax.fori_loop(0, B // 512, make_yt, 0)
    cp_p.wait()

    lane = lax.broadcasted_iota(jnp.int32, (DIMS // 2, 128), 1)

    def build_x(c):
        def wait_block(j, _):
            g = owner(c, j)

            @pl.when(g != me)
            def _():
                pltpu.make_async_remote_copy(
                    src_ref=xown, dst_ref=xall.at[g], send_sem=xs_sem.at[0], recv_sem=xr_sem.at[g],
                    device_id=group_id((me + 1) % GROUP), device_id_type=MESH,
                ).wait_recv()

            return 0

        lax.fori_loop(0, NZ, wait_block, 0)
        for pair in range(NZ // 2):
            va = xall[owner(c, 2 * pair)].astype(F32)
            vb = xall[owner(c, 2 * pair + 1)].astype(F32)
            even = jnp.where(lane < 64, va, pltpu.roll(vb, 64, 1))
            odd = jnp.where(lane < 64, pltpu.roll(va, 64, 1), vb)
            xv = jnp.concatenate([even, odd], axis=0)
            nh, nm, nl = split3(-alpha * jnp.sum(xv * xv, axis=0, keepdims=True))
            r = lax.broadcasted_iota(jnp.int32, (DIMS, 128), 0)
            extra = jnp.where(
                r == 0, nh,
                jnp.where(r == 1, nm, jnp.where(r == 2, nl, jnp.where(r < 6, 1.0, 0.0))),
            )
            whole = jnp.concatenate([xv, xv, xv, extra], axis=0).astype(BF16)
            xaug[:, pair * 128 : (pair + 1) * 128] = whole

    def rs_copy(c, j):
        g = owner(c, j)
        return pltpu.make_async_remote_copy(
            src_ref=spart.at[c, pl.ds(pl.multiple_of(j * 8, 8), 8), :],
            dst_ref=rsrecv.at[(me - g + GROUP) % GROUP - 1],
            send_sem=rs_s.at[c * NZ + j],
            recv_sem=rs_r.at[(me - g + GROUP) % GROUP - 1],
            device_id=group_id(g),
            device_id_type=MESH,
        )

    def ag_copy(r):
        rows = pl.ds(pl.multiple_of(z * 8, 8), 8)
        return pltpu.make_async_remote_copy(
            src_ref=sfull.at[my_chunk, rows, :],
            dst_ref=sfull.at[my_chunk, rows, :],
            send_sem=ag_s.at[r - 1],
            recv_sem=ag_r.at[my_chunk * NZ + z],
            device_id=group_id((me + r) % GROUP),
            device_id_type=MESH,
        )

    def reduce_own(c):
        @pl.when(my_chunk == c)
        def _():
            rows = pl.ds(pl.multiple_of(z * 8, 8), 8)

            def add(i, total):
                pltpu.make_async_remote_copy(
                    src_ref=rsrecv.at[i], dst_ref=rsrecv.at[i], send_sem=rs_s.at[0], recv_sem=rs_r.at[i],
                    device_id=group_id((me + 1) % GROUP), device_id_type=MESH,
                ).wait_recv()
                return total + rsrecv[i]

            sfull[c, rows, :] = lax.fori_loop(0, GROUP - 1, add, spart[c, rows, :])

            def send(r, _):
                ag_copy(r).start()
                return 0

            lax.fori_loop(1, GROUP, send, 0)

    def phase1(c, _):
        build_x(c)

        def tile(i, total):
            b0 = pl.multiple_of(i * TB, TB)
            t = lax.dot_general(yt[pl.ds(b0, TB), :], xaug[...], NN, preferred_element_type=F32)
            k = jnp.exp2(t).astype(BF16)
            kmat[pl.ds(b0, TB), pl.ds(pl.multiple_of(c * CA, CA), CA)] = k
            return total + lax.dot_general(
                probes[:, pl.ds(b0, TB)], k, NN, preferred_element_type=F32
            )[:PROBES]

        spart[c] = lax.fori_loop(0, B // TB, tile, jnp.zeros((PROBES, CA), F32))

        def send(j, _):
            @pl.when(owner(c, j) != me)
            def _():
                rs_copy(c, j).start()

            return 0

        lax.fori_loop(0, NZ, send, 0)

        @pl.when(c > 0)
        def _():
            reduce_own(c - 1)

        return 0

    lax.fori_loop(0, CHUNKS, phase1, 0)
    reduce_own(CHUNKS - 1)

    gsend[...] = jnp.zeros((PROBES, 128), F32)

    def take_chunk(c, g):
        def wait_piece(j, _):
            @pl.when(owner(c, j) != me)
            def _():
                rows = pl.ds(pl.multiple_of(j * 8, 8), 8)
                pltpu.make_async_remote_copy(
                    src_ref=sfull.at[c, rows, :], dst_ref=sfull.at[c, rows, :],
                    send_sem=ag_s.at[0], recv_sem=ag_r.at[c * NZ + j],
                    device_id=group_id((me + 1) % GROUP), device_id_type=MESH,
                ).wait_recv()

            return 0

        lax.fori_loop(0, NZ, wait_piece, 0)
        s = sfull[c]
        hi = s.astype(BF16).astype(F32)
        st[pl.ds(pl.multiple_of(c * CA, CA), CA), :] = jnp.transpose(
            jnp.concatenate([hi, s - hi], axis=0)
        ).astype(BF16)
        return g + lax.dot_general(s, s, NT, precision=HIGHEST, preferred_element_type=F32)

    gsend[:, 0:PROBES] = lax.fori_loop(0, CHUNKS, take_chunk, jnp.zeros((PROBES, PROBES), F32))

    def g_copy(r):
        return pltpu.make_async_remote_copy(
            src_ref=gsend, dst_ref=grecv.at[r - 1], send_sem=g_s.at[r - 1], recv_sem=g_r.at[r - 1],
            device_id=peer_id((mine + r) % PEERS), device_id_type=MESH,
        )

    def g_start(r, _):
        g_copy(r).start()
        return 0

    lax.fori_loop(1, PEERS, g_start, 0)

    wide = lax.broadcasted_iota(jnp.int32, (OWN // 2, 128), 1)

    def image_part(o):
        zt = lax.dot_general(
            kmat[pl.ds(pl.multiple_of(o * OWN, OWN), OWN), :], st[...], NN, preferred_element_type=F32
        )
        u = zt + pltpu.roll(zt, 64, 1)
        return jnp.where(wide < 64, u[: OWN // 2], u[OWN // 2 :])

    def zc_copy(t):
        return pltpu.make_async_remote_copy(
            src_ref=zsend.at[t], dst_ref=zcrecv.at[t], send_sem=zc_s.at[t], recv_sem=zc_r.at[t],
            device_id=peer_id(y * 2 + 1 - core), device_id_type=MESH,
        )

    def zy_copy(t):
        return pltpu.make_async_remote_copy(
            src_ref=zmine.at[t], dst_ref=zyrecv.at[t], send_sem=zy_s.at[t], recv_sem=zy_r.at[t],
            device_id=peer_id(((y + 1 + t) % NY) * 2 + core), device_id_type=MESH,
        )

    def phase2(t, _):
        yo = (y + 1 + t) % NY
        zsend[t] = image_part(yo * 2 + 1 - core)
        zc_copy(t).start()
        own = image_part(yo * 2 + core)
        zc_copy(t).wait_recv()
        zmine[t] = own + zcrecv[t]

        @pl.when(t < NY - 1)
        def _():
            zy_copy(t).start()

        return 0

    lax.fori_loop(0, NY, phase2, 0)

    def g_wait(r, total):
        g_copy(r).wait()
        return total + grecv[r - 1]

    gsum_ref[...] = lax.fori_loop(1, PEERS, g_wait, gsend[...])
    tile = sfull[my_chunk, :, pl.ds(pl.multiple_of((z // 2) * 128, 128), 128)]
    sown_ref[...] = jnp.where(z % 2 == 1, pltpu.roll(tile, 64, 1), tile)

    def xs_wait(r, _):
        slab_copy(r).wait_send()
        ag_copy(r).wait_send()
        return 0

    lax.fori_loop(1, GROUP, xs_wait, 0)

    def rs_wait(i, _):
        c = i // NZ
        j = i % NZ

        @pl.when(owner(c, j) != me)
        def _():
            rs_copy(c, j).wait_send()

        return 0

    lax.fori_loop(0, CHUNKS * NZ, rs_wait, 0)

    def zc_wait(t, _):
        zc_copy(t).wait_send()
        return 0

    lax.fori_loop(0, NY, zc_wait, 0)

    def zy_wait(t, total):
        zy_copy(t).wait()
        return total + zyrecv[t]

    zsum_ref[...] = lax.fori_loop(0, NY - 1, zy_wait, zmine[NY - 1])


def final_kernel(zsum_ref, gsum_ref, sown_ref, basis_ref, image_ref, *, slab_total, point_total):
    lane = lax.broadcasted_iota(jnp.int32, (PROBES, 128), 1)
    rows = lax.broadcasted_iota(jnp.int32, (PROBES, 128), 0)
    gram = gsum_ref[...] / slab_total
    diag = jnp.where(lane == rows, gram, 0.0)
    trace = jnp.sum(diag)
    m = jnp.where(lane < 64, gram, jnp.where(lane - 64 == rows, 1.0, 0.0))
    for k in range(PROBES - 1):
        pivot = m[k : k + 1, :]
        factor = m[:, k : k + 1] / m[k : k + 1, k : k + 1]
        m = m - jnp.where(rows > k, factor * pivot, 0.0)
    d = jnp.sum(jnp.where(lane == rows, m, 0.0), axis=1, keepdims=True)
    upper = jnp.where(lane >= 64, m / jnp.sqrt(d), 0.0)
    lower = pltpu.roll(upper, 64, 1)
    basis = lax.dot_general(
        lower[:, :64], sown_ref[...], NN, precision=HIGHEST, preferred_element_type=F32
    )
    basis_ref[...] = basis[:, :64].astype(BF16)
    scale = jnp.sqrt(jnp.float32(PROBES * point_total) / jnp.full((1, 1), trace)) / slab_total
    zs = zsum_ref[...]
    for half, w in ((0, lower), (1, upper)):
        image_ref[:, half * 512 : half * 512 + 512] = scale * lax.dot_general(
            w, zs, NT, precision=HIGHEST, preferred_element_type=F32
        )


def body(slab_points, col_points, probes):
    vmem = pl.BlockSpec(memory_space=pltpu.VMEM)
    dma = pltpu.SemaphoreType.DMA
    zsum, gsum, sown = pl.pallas_call(
        main_kernel,
        out_shape=(
            jax.ShapeDtypeStruct((OWN // 2, 128), F32),
            jax.ShapeDtypeStruct((PROBES, 128), F32),
            jax.ShapeDtypeStruct((PROBES, 128), F32),
        ),
        in_specs=[vmem, pl.BlockSpec(memory_space=pl.ANY), pl.BlockSpec(memory_space=pl.ANY)],
        out_specs=(vmem, vmem, vmem),
        scratch_shapes=[
            pltpu.VMEM((DIMS, B), BF16),
            pltpu.VMEM((128, B), BF16),
            pltpu.VMEM((B, 256), BF16),
            pltpu.VMEM((GROUP, 32, 128), BF16),
            pltpu.VMEM((256, CA), BF16),
            pltpu.VMEM((B, A), BF16),
            pltpu.VMEM((CHUNKS, PROBES, CA), F32),
            pltpu.VMEM((GROUP - 1, 8, CA), F32),
            pltpu.VMEM((CHUNKS, PROBES, CA), F32),
            pltpu.VMEM((A, 128), BF16),
            pltpu.VMEM((NY, OWN // 2, 128), F32),
            pltpu.VMEM((NY, OWN // 2, 128), F32),
            pltpu.VMEM((NY, OWN // 2, 128), F32),
            pltpu.VMEM((NY - 1, OWN // 2, 128), F32),
            pltpu.VMEM((PROBES, 128), F32),
            pltpu.VMEM((PEERS - 1, PROBES, 128), F32),
            pltpu.VMEM((32, 128), BF16),
            dma((2,)),
            dma((GROUP - 1,)),
            dma((GROUP,)),
            dma((CHUNKS * NZ,)),
            dma((GROUP - 1,)),
            dma((GROUP - 1,)),
            dma((CHUNKS * NZ,)),
            dma((NY,)),
            dma((NY,)),
            dma((NY - 1,)),
            dma((NY - 1,)),
            dma((PEERS - 1,)),
            dma((PEERS - 1,)),
        ],
        compiler_params=pltpu.CompilerParams(
            collective_id=0, has_side_effects=True, vmem_limit_bytes=62 << 20
        ),
        name="slab_kernel",
    )(slab_points, col_points, probes)
    return pl.pallas_call(
        functools.partial(final_kernel, slab_total=16384, point_total=262144),
        out_shape=(
            jax.ShapeDtypeStruct((PROBES, BLK), BF16),
            jax.ShapeDtypeStruct((PROBES, OWN), F32),
        ),
        in_specs=[vmem, vmem, vmem],
        out_specs=(vmem, vmem),
        name="factor_and_image",
    )(zsum, gsum, sown)


def solution(mesh):
    return jax.shard_map(
        body,
        mesh=mesh,
        in_specs=(P(None, ("row", "col")), P(None, "col"), P(None, "col")),
        out_specs=(P(None, ("row", "col")), P(None, ("col", "row"))),
        check_vma=False,
    )
```

```python
import functools
import math

import jax
import jax.numpy as jnp
from jax import lax
from jax.experimental import pallas as pl
from jax.experimental.pallas import tpu as pltpu
from jax.sharding import PartitionSpec as P

F32 = jnp.float32
BF16 = jnp.bfloat16
MESH = pl.DeviceIdType.MESH
NN = (((1,), (0,)), ((), ()))
NT = (((1,), (1,)), ((), ()))
LOG2E = 1.4426950408889634
HIGHEST = lax.Precision.HIGHEST

NX, NZ, NY, NCORE = 4, 8, 4, 2
GROUP = NX * NZ
PEERS = NY * NCORE
DIMS = 64
PROBES = 64
BLK = 64
CHUNKS = 4
CA = 512
A = CHUNKS * CA
B = 8192
TB = 4096
OWN = 1024


def split3(v):
    h = v.astype(BF16).astype(F32)
    m = (v - h).astype(BF16).astype(F32)
    return h, m, v - h - m


def main_kernel(
    slab_ref, col_ref, probe_ref,
    zsum_ref, lower_ref, trace_ref, sown_ref,
    cols, probes, yt, xall, xaug, kmat, spart, rsrecv, sfull, st,
    zsend, zmine, zcrecv, zyrecv, gsend, grecv,
    in_sem, sz_s, sz_r, sx_s, sx_r, rs_s, rs_r, ag_s, ag_r,
    zc_s, zc_r, zy_s, zy_r, g_s, g_r,
    *, slab_total,
):
    row = lax.axis_index("row")
    col = lax.axis_index("col")
    core = row % 2
    y = (row // 2) % 4
    zhi = row // 8
    z = zhi * 4 + col % 4
    x = col // 4
    mine = y * NCORE + core

    def at_z(r):
        gz = (z + r) % NZ
        return ((gz // 4) * 8 + mine, x * 4 + gz % 4)

    def at_x(r):
        return (row, ((x + r) % NX) * 4 + col % 4)

    me = z * NX + x

    def at_group(g):
        gz = g // NX
        return ((gz // 4) * 8 + mine, (g % NX) * 4 + gz % 4)

    def at_peer(q):
        return (zhi * 8 + q, col)

    def each(lo, hi, f):
        def step(r, _):
            f(r)
            return 0

        lax.fori_loop(lo, hi, step, 0)

    def remote(src, dst, send, recv, device):
        return pltpu.make_async_remote_copy(
            src_ref=src, dst_ref=dst, send_sem=send, recv_sem=recv, device_id=device, device_id_type=MESH
        )

    cp_c = pltpu.make_async_copy(col_ref.at[:, pl.ds(pl.multiple_of(zhi * B, B), B)], cols, in_sem.at[0])
    cp_p = pltpu.make_async_copy(
        probe_ref.at[:, pl.ds(pl.multiple_of(zhi * B, B), B)], probes.at[pl.ds(0, PROBES), :], in_sem.at[1]
    )
    cp_c.start()
    cp_p.start()

    barrier = pltpu.get_barrier_semaphore()

    def greet(device):
        pl.semaphore_signal(barrier, inc=1, device_id=device, device_id_type=MESH)

    each(1, GROUP, lambda r: greet(at_group((me + r) % GROUP)))
    each(1, PEERS, lambda r: greet(at_peer((mine + r) % PEERS)))

    s_in = slab_ref[...].astype(F32)
    xall[x, z] = jnp.concatenate([s_in[: DIMS // 2], s_in[DIMS // 2 :]], axis=1).astype(BF16)
    probes[PROBES:, :] = jnp.zeros((128 - PROBES, B), BF16)

    pl.semaphore_wait(barrier, GROUP - 1 + PEERS - 1)

    def slab_z(r):
        return remote(xall.at[x, z], xall.at[x, z], sz_s.at[r - 1], sz_r.at[r - 1], at_z(r))

    def slab_x(r):
        return remote(xall.at[x], xall.at[x], sx_s.at[r - 1], sx_r.at[r - 1], at_x(r))

    each(1, NZ, lambda r: slab_z(r).start())

    cp_c.wait()
    alpha = LOG2E * 8.0 / DIMS

    def make_yt(i):
        b0 = pl.multiple_of(i * 512, 512)
        yv = cols[:, pl.ds(b0, 512)].astype(F32)
        yp = yv * (2.0 * alpha)
        h, m, l = split3(yp)
        nh, nm, nl = split3(-alpha * jnp.sum(yv * yv, axis=0, keepdims=True))
        r = lax.broadcasted_iota(jnp.int32, (DIMS, 512), 0)
        extra = jnp.where(
            r < 3, 1.0, jnp.where(r == 3, nh, jnp.where(r == 4, nm, jnp.where(r == 5, nl, 0.0)))
        )
        yt[pl.ds(b0, 512), 0:128] = jnp.transpose(jnp.concatenate([h, m], axis=0)).astype(BF16)
        yt[pl.ds(b0, 512), 128:256] = jnp.transpose(jnp.concatenate([l, extra], axis=0)).astype(BF16)

    each(0, B // 1024, make_yt)
    each(1, NZ, lambda r: slab_z(r).wait_recv())
    each(1, NX, lambda r: slab_x(r).start())
    each(B // 1024, B // 512, make_yt)
    cp_p.wait()
    lane = lax.broadcasted_iota(jnp.int32, (DIMS // 2, 128), 1)

    def build_x(c):
        for pair in range(NZ // 2):
            va = xall[c, 2 * pair].astype(F32)
            vb = xall[c, 2 * pair + 1].astype(F32)
            even = jnp.where(lane < 64, va, pltpu.roll(vb, 64, 1))
            odd = jnp.where(lane < 64, pltpu.roll(va, 64, 1), vb)
            xv = jnp.concatenate([even, odd], axis=0)
            nh, nm, nl = split3(-alpha * jnp.sum(xv * xv, axis=0, keepdims=True))
            r = lax.broadcasted_iota(jnp.int32, (DIMS, 128), 0)
            extra = jnp.where(
                r == 0, nh,
                jnp.where(r == 1, nm, jnp.where(r == 2, nl, jnp.where(r < 6, 1.0, 0.0))),
            )
            whole = jnp.concatenate([xv, xv, xv, extra], axis=0).astype(BF16)
            xaug[:, pair * 128 : (pair + 1) * 128] = whole

    def piece(g):
        return (
            pl.ds(pl.multiple_of((g // 4) * 8, 8), 8),
            pl.ds(pl.multiple_of((g % 4) * 128, 128), 128),
        )

    def rs(c, r):
        g = (me + r) % GROUP
        return remote(
            spart.at[(c, *piece(g))], rsrecv.at[c, r - 1], rs_s.at[c], rs_r.at[c], at_group(g)
        )

    def ag(c, r):
        here = sfull.at[(c, *piece(me))]
        return remote(here, here, ag_s.at[c], ag_r.at[c], at_group((me + r) % GROUP))

    def rs_all(c):
        return remote(rsrecv.at[c], rsrecv.at[c], rs_s.at[c], rs_r.at[c], at_z(1))

    def ag_all(c):
        return remote(rsrecv.at[c], rsrecv.at[c], ag_s.at[c], ag_r.at[c], at_z(1))

    def reduce_own(c):
        rs_all(c).wait_recv()
        sfull[(c, *piece(me))] = spart[(c, *piece(me))] + jnp.sum(rsrecv[c], axis=0)
        each(1, GROUP, lambda r: ag(c, r).start())

    def chunk_at(c):
        return pl.ds(pl.multiple_of(c * CA, CA), CA)

    def tile(c, i):
        b0 = pl.multiple_of(i * TB, TB)
        t = lax.dot_general(yt[pl.ds(b0, TB), :], xaug[...], NN, preferred_element_type=F32)
        k = jnp.exp2(t).astype(BF16)
        kmat[pl.ds(b0, TB), chunk_at(c)] = k
        return lax.dot_general(probes[:, pl.ds(b0, TB)], k, NN, preferred_element_type=F32)[:PROBES]

    def clear_part(c):
        spart[c] = jnp.zeros((PROBES, CA), F32)

    each(0, CHUNKS, clear_part)

    def phase1(n):
        index = jnp.where(n == 0, 2 * x, jnp.where(n <= 2 * x, n - 1, n))
        c = index // 2
        half = index % 2

        @pl.when((half == 0) & (c != x))
        def _():
            slab_x((x - c + NX) % NX).wait_recv()

        build_x(c)
        spart[c] += tile(c, half)
        pl.when(half == 1)(lambda: each(1, GROUP, lambda r: rs(c, r).start()))
        pl.when(n == 6)(lambda: reduce_own(0))

    each(0, 2 * CHUNKS, phase1)
    reduce_own(1)
    reduce_own(2)

    wide = lax.broadcasted_iota(jnp.int32, (OWN // 2, 128), 1)
    gsend[...] = jnp.zeros((PROBES, 128), F32)

    def take_chunk(c):
        ag_all(c).wait_recv()
        s = sfull[c]
        hi = s.astype(BF16).astype(F32)
        st[...] = jnp.transpose(jnp.concatenate([hi, s - hi], axis=0)).astype(BF16)
        gsend[:, 0:PROBES] += lax.dot_general(s, s, NT, precision=HIGHEST, preferred_element_type=F32)

    def image_part(c, o):
        zt = lax.dot_general(
            kmat[pl.ds(pl.multiple_of(o * OWN, OWN), OWN), chunk_at(c)], st[...], NN,
            preferred_element_type=F32,
        )
        u = zt + pltpu.roll(zt, 64, 1)
        return jnp.where(wide < 64, u[: OWN // 2], u[OWN // 2 :])

    def both(c, t):
        yo = (y + 1 + t) % NY
        zsend[t] += image_part(c, yo * 2 + 1 - core)
        zmine[t] += image_part(c, yo * 2 + core)

    def clear(t):
        zsend[t] = jnp.zeros((OWN // 2, 128), F32)
        zmine[t] = jnp.zeros((OWN // 2, 128), F32)

    each(0, NY, clear)

    def one_pass(c):
        take_chunk(c)
        each(0, 2, lambda t: both(c, t))
        pl.when(c == 0)(lambda: reduce_own(3))
        each(2, NY, lambda t: both(c, t))

    each(0, CHUNKS - 1, one_pass)
    take_chunk(CHUNKS - 1)

    def g_copy(r):
        return remote(
            gsend, grecv.at[r - 1], g_s.at[r - 1], g_r.at[r - 1], at_peer((mine + r) % PEERS)
        )

    each(1, PEERS, lambda r: g_copy(r).start())

    def zc(t):
        return remote(zsend.at[t], zcrecv.at[t], zc_s.at[t], zc_r.at[t], at_peer(y * 2 + 1 - core))

    def zy(t):
        return remote(
            zmine.at[t], zyrecv.at[t], zy_s.at[t], zy_r.at[t], at_peer(((y + 1 + t) % NY) * 2 + core)
        )

    def last_pass(t):
        yo = (y + 1 + t) % NY
        zsend[t] += image_part(CHUNKS - 1, yo * 2 + 1 - core)
        zc(t).start()
        own = image_part(CHUNKS - 1, yo * 2 + core)
        zc(t).wait_recv()
        zmine[t] += own + zcrecv[t]
        pl.when(t < NY - 1)(lambda: zy(t).start())

    each(0, NY, last_pass)

    each(1, PEERS, lambda r: g_copy(r).wait_send())
    each(1, PEERS, lambda r: g_copy(r).wait_recv())
    total = gsend[...]
    for r in range(PEERS - 1):
        total = total + grecv[r]
    gram = total / slab_total
    glane = lax.broadcasted_iota(jnp.int32, (PROBES, 128), 1)
    grow = lax.broadcasted_iota(jnp.int32, (PROBES, 128), 0)
    trace_ref[...] = jnp.full((8, 128), jnp.sum(jnp.where(glane == grow, gram, 0.0)))
    m = jnp.where(glane < 64, gram, jnp.where(glane - 64 == grow, 1.0, 0.0))
    for k in range(PROBES - 1):
        pivot = m[k : k + 1, :]
        factor = m[:, k : k + 1] / m[k : k + 1, k : k + 1]
        m = m - jnp.where(grow > k, factor * pivot, 0.0)
    d = jnp.sum(jnp.where(glane == grow, m, 0.0), axis=1, keepdims=True)
    lower_ref[...] = jnp.where(glane >= 64, m / jnp.sqrt(d), 0.0)

    own_lanes = pl.ds(pl.multiple_of((z // 2) * 128, 128), 128)
    stile = sfull[x, :, own_lanes]
    sown_ref[...] = jnp.where(z % 2 == 1, pltpu.roll(stile, 64, 1), stile)

    each(1, NZ, lambda r: slab_z(r).wait_send())
    each(1, NX, lambda r: slab_x(r).wait_send())

    each(0, CHUNKS, lambda c: rs_all(c).wait_send())
    each(0, CHUNKS, lambda c: ag_all(c).wait_send())
    each(0, NY, lambda t: zc(t).wait_send())
    each(0, NY - 1, lambda t: zy(t).wait())
    zsum_ref[...] = zmine[NY - 1] + (zyrecv[0] + zyrecv[1] + zyrecv[2])


def final_kernel(zsum_ref, upper_ref, trace_ref, sown_ref, basis_ref, image_ref, *, slab_total, point_total):
    upper = upper_ref[...]
    lower = pltpu.roll(upper, 64, 1)
    basis = lax.dot_general(
        lower[:, :64], sown_ref[...], NN, precision=HIGHEST, preferred_element_type=F32
    )
    basis_ref[...] = basis[:, :64].astype(BF16)
    scale = jnp.sqrt(jnp.float32(PROBES * point_total) / trace_ref[0:1, 0:1]) / slab_total
    zs = zsum_ref[...]
    for half, w in ((0, lower), (1, upper)):
        image_ref[:, half * 512 : half * 512 + 512] = scale * lax.dot_general(
            w, zs, NT, precision=HIGHEST, preferred_element_type=F32
        )


def body(slab_points, col_points, probes):
    vmem = pl.BlockSpec(memory_space=pltpu.VMEM)
    hbm = pl.BlockSpec(memory_space=pl.ANY)
    dma = pltpu.SemaphoreType.DMA
    zsum, lower, trace, sown = pl.pallas_call(
        functools.partial(main_kernel, slab_total=A * PEERS),
        out_shape=(
            jax.ShapeDtypeStruct((OWN // 2, 128), F32),
            jax.ShapeDtypeStruct((PROBES, 128), F32),
            jax.ShapeDtypeStruct((8, 128), F32),
            jax.ShapeDtypeStruct((PROBES, 128), F32),
        ),
        in_specs=[vmem, hbm, hbm],
        out_specs=(vmem, vmem, vmem, vmem),
        scratch_shapes=[
            pltpu.VMEM((DIMS, B), BF16),
            pltpu.VMEM((128, B), BF16),
            pltpu.VMEM((B, 256), BF16),
            pltpu.VMEM((NX, NZ, 32, 128), BF16),
            pltpu.VMEM((256, CA), BF16),
            pltpu.VMEM((B, A), BF16),
            pltpu.VMEM((CHUNKS, PROBES, CA), F32),
            pltpu.VMEM((CHUNKS, GROUP - 1, 8, 128), F32),
            pltpu.VMEM((CHUNKS, PROBES, CA), F32),
            pltpu.VMEM((CA, 128), BF16),
            pltpu.VMEM((NY, OWN // 2, 128), F32),
            pltpu.VMEM((NY, OWN // 2, 128), F32),
            pltpu.VMEM((NY, OWN // 2, 128), F32),
            pltpu.VMEM((NY - 1, OWN // 2, 128), F32),
            pltpu.VMEM((PROBES, 128), F32),
            pltpu.VMEM((PEERS - 1, PROBES, 128), F32),
            dma((2,)),
            dma((NZ - 1,)), dma((NZ - 1,)), dma((NX - 1,)), dma((NX - 1,)),
            dma((CHUNKS,)), dma((CHUNKS,)), dma((CHUNKS,)), dma((CHUNKS,)),
            dma((NY,)), dma((NY,)), dma((NY - 1,)), dma((NY - 1,)),
            dma((PEERS - 1,)), dma((PEERS - 1,)),
        ],
        compiler_params=pltpu.CompilerParams(
            collective_id=0, has_side_effects=True, vmem_limit_bytes=62 << 20
        ),
        name="slab_kernel",
    )(slab_points, col_points, probes)
    return pl.pallas_call(
        functools.partial(final_kernel, slab_total=A * PEERS, point_total=B * GROUP),
        out_shape=(
            jax.ShapeDtypeStruct((PROBES, BLK), BF16),
            jax.ShapeDtypeStruct((PROBES, OWN), F32),
        ),
        in_specs=[vmem, vmem, vmem, vmem],
        out_specs=(vmem, vmem),
        name="image_kernel",
    )(zsum, lower, trace, sown)


def solution(mesh):
    return jax.shard_map(
        body,
        mesh=mesh,
        in_specs=(P(None, ("row", "col")), P(None, "col"), P(None, "col")),
        out_specs=(P(None, ("row", "col")), P(None, ("col", "row"))),
        check_vma=False,
    )
```

```python
import functools
import math

import jax
import jax.numpy as jnp
from jax import lax
from jax.experimental import pallas as pl
from jax.experimental.pallas import tpu as pltpu
from jax.sharding import PartitionSpec as P

F32 = jnp.float32
BF16 = jnp.bfloat16
MESH = pl.DeviceIdType.MESH
NN = (((1,), (0,)), ((), ()))
NT = (((1,), (1,)), ((), ()))
LOG2E = 1.4426950408889634
HIGHEST = lax.Precision.HIGHEST

NX, NZ, NY, NCORE = 4, 8, 4, 2
GROUP = NX * NZ
PEERS = NY * NCORE
DIMS = 64
PROBES = 64
BLK = 64
CHUNKS = 4
CA = 512
A = CHUNKS * CA
B = 8192
TB = 4096
OWN = 1024


def split3(v):
    h = v.astype(BF16).astype(F32)
    m = (v - h).astype(BF16).astype(F32)
    return h, m, v - h - m


def main_kernel(
    slab_ref, col_ref, probe_ref,
    basis_ref, image_ref,
    cols, probes, yt, xall, xaug, kmat, spart, rsrecv, sfull, st,
    zacc, zsend, zmine, zcrecv, zout, zyrecv, gacc, gall, tmat, tinv,
    in_sem, sz_s, sz_r, sx_s, sx_r, rs_s, rs_r, ag_s, ag_r,
    zc_s, zc_r, zy_s, zy_r, g_s, g_r,
    *, slab_total, point_total,
):
    row = lax.axis_index("row")
    col = lax.axis_index("col")
    core = row % 2
    y = (row // 2) % 4
    zhi = row // 8
    z = zhi * 4 + col % 4
    x = col // 4
    mine = y * NCORE + core

    def at_z(r):
        gz = (z + r) % NZ
        return ((gz // 4) * 8 + mine, x * 4 + gz % 4)

    def at_x(r):
        return (row, ((x + r) % NX) * 4 + col % 4)

    me = z * NX + x

    def at_group(g):
        gz = g // NX
        return ((gz // 4) * 8 + mine, (g % NX) * 4 + gz % 4)

    def at_peer(q):
        return (zhi * 8 + q, col)

    def each(lo, hi, f):
        def step(r, _):
            f(r)
            return 0

        lax.fori_loop(lo, hi, step, 0)

    def remote(src, dst, send, recv, device):
        return pltpu.make_async_remote_copy(
            src_ref=src, dst_ref=dst, send_sem=send, recv_sem=recv, device_id=device, device_id_type=MESH
        )

    cp_c = pltpu.make_async_copy(col_ref.at[:, pl.ds(pl.multiple_of(zhi * B, B), B)], cols, in_sem.at[0])
    cp_p = pltpu.make_async_copy(
        probe_ref.at[:, pl.ds(pl.multiple_of(zhi * B, B), B)], probes.at[pl.ds(0, PROBES), :], in_sem.at[1]
    )
    cp_c.start()
    cp_p.start()

    barrier = pltpu.get_barrier_semaphore()

    def greet(device):
        pl.semaphore_signal(barrier, inc=1, device_id=device, device_id_type=MESH)

    each(1, GROUP, lambda r: greet(at_group((me + r) % GROUP)))
    each(1, PEERS, lambda r: greet(at_peer((mine + r) % PEERS)))

    s_in = slab_ref[...].astype(F32)
    xall[x, z] = jnp.concatenate([s_in[: DIMS // 2], s_in[DIMS // 2 :]], axis=1).astype(BF16)
    probes[PROBES:, :] = jnp.zeros((128 - PROBES, B), BF16)

    pl.semaphore_wait(barrier, GROUP - 1 + PEERS - 1)

    def slab_z(r):
        return remote(xall.at[x, z], xall.at[x, z], sz_s.at[r - 1], sz_r.at[r - 1], at_z(r))

    def slab_x(r):
        return remote(xall.at[x], xall.at[x], sx_s.at[r - 1], sx_r.at[r - 1], at_x(r))

    each(1, NZ, lambda r: slab_z(r).start())

    cp_c.wait()
    alpha = LOG2E * 8.0 / DIMS

    def make_yt(i):
        b0 = pl.multiple_of(i * 512, 512)
        yv = cols[:, pl.ds(b0, 512)].astype(F32)
        yp = yv * (2.0 * alpha)
        h, m, l = split3(yp)
        nh, nm, nl = split3(-alpha * jnp.sum(yv * yv, axis=0, keepdims=True))
        r = lax.broadcasted_iota(jnp.int32, (DIMS, 512), 0)
        extra = jnp.where(
            r < 3, 1.0, jnp.where(r == 3, nh, jnp.where(r == 4, nm, jnp.where(r == 5, nl, 0.0)))
        )
        yt[pl.ds(b0, 512), 0:128] = jnp.transpose(jnp.concatenate([h, m], axis=0)).astype(BF16)
        yt[pl.ds(b0, 512), 128:256] = jnp.transpose(jnp.concatenate([l, extra], axis=0)).astype(BF16)

    each(0, B // 1024, make_yt)
    each(1, NZ, lambda r: slab_z(r).wait_recv())
    each(1, NX, lambda r: slab_x(r).start())
    each(B // 1024, B // 512, make_yt)
    cp_p.wait()

    lane = lax.broadcasted_iota(jnp.int32, (DIMS // 2, 128), 1)

    def build_x(c):
        for pair in range(NZ // 2):
            va = xall[c, 2 * pair].astype(F32)
            vb = xall[c, 2 * pair + 1].astype(F32)
            even = jnp.where(lane < 64, va, pltpu.roll(vb, 64, 1))
            odd = jnp.where(lane < 64, pltpu.roll(va, 64, 1), vb)
            xv = jnp.concatenate([even, odd], axis=0)
            nh, nm, nl = split3(-alpha * jnp.sum(xv * xv, axis=0, keepdims=True))
            r = lax.broadcasted_iota(jnp.int32, (DIMS, 128), 0)
            extra = jnp.where(
                r == 0, nh,
                jnp.where(r == 1, nm, jnp.where(r == 2, nl, jnp.where(r < 6, 1.0, 0.0))),
            )
            whole = jnp.concatenate([xv, xv, xv, extra], axis=0).astype(BF16)
            xaug[:, pair * 128 : (pair + 1) * 128] = whole

    def piece(g):
        return (
            pl.ds(pl.multiple_of((g // 4) * 8, 8), 8),
            pl.ds(pl.multiple_of((g % 4) * 128, 128), 128),
        )

    def rs(c, r):
        g = (me + r) % GROUP
        return remote(
            spart.at[(c, *piece(g))], rsrecv.at[c, r - 1], rs_s.at[c], rs_r.at[c], at_group(g)
        )

    def ag(c, r):
        here = sfull.at[(c, *piece(me))]
        return remote(here, here, ag_s.at[c], ag_r.at[c], at_group((me + r) % GROUP))

    def rs_all(c):
        return remote(rsrecv.at[c], rsrecv.at[c], rs_s.at[c], rs_r.at[c], at_z(1))

    def ag_all(c):
        return remote(rsrecv.at[c], rsrecv.at[c], ag_s.at[c], ag_r.at[c], at_z(1))

    def reduce_own(c):
        rs_all(c).wait_recv()
        sfull[(c, *piece(me))] = spart[(c, *piece(me))] + jnp.sum(rsrecv[c], axis=0)
        each(1, GROUP, lambda r: ag(c, r).start())

    def chunk_at(c):
        return pl.ds(pl.multiple_of(c * CA, CA), CA)

    def tile(c, i):
        b0 = pl.multiple_of(i * TB, TB)
        t = lax.dot_general(yt[pl.ds(b0, TB), :], xaug[...], NN, preferred_element_type=F32)
        k = jnp.exp2(t).astype(BF16)
        kmat[pl.ds(b0, TB), chunk_at(c)] = k
        return lax.dot_general(probes[:, pl.ds(b0, TB)], k, NN, preferred_element_type=F32)[:PROBES]

    def clear_part(c):
        spart[c] = jnp.zeros((PROBES, CA), F32)

    each(0, CHUNKS, clear_part)

    def phase1(n):
        index = jnp.where(n == 0, 2 * x, jnp.where(n <= 2 * x, n - 1, n))
        c = index // 2
        half = index % 2

        @pl.when((half == 0) & (c != x))
        def _():
            slab_x((x - c + NX) % NX).wait_recv()

        build_x(c)
        spart[c] += tile(c, half)
        pl.when(half == 1)(lambda: each(1, GROUP, lambda r: rs(c, r).start()))
        pl.when(n == 6)(lambda: reduce_own(0))

    each(0, 2 * CHUNKS, phase1)
    each(1, CHUNKS, reduce_own)

    wide = lax.broadcasted_iota(jnp.int32, (OWN // 2, 128), 1)
    glane = lax.broadcasted_iota(jnp.int32, (PROBES, 128), 1)
    grow = lax.broadcasted_iota(jnp.int32, (PROBES, 128), 0)
    gacc[...] = jnp.zeros((PROBES, 128), F32)

    def take_chunk(c):
        ag_all(c).wait_recv()
        s = sfull[c]
        hi = s.astype(BF16).astype(F32)
        st[...] = jnp.transpose(jnp.concatenate([hi, s - hi], axis=0)).astype(BF16)

    def add_gram(c):
        s = sfull[c]
        gacc[:, 0:PROBES] += lax.dot_general(s, s, NT, precision=HIGHEST, preferred_element_type=F32)

    def g_copy(p, r):
        return remote(
            gall.at[p, mine], gall.at[p, mine], g_s.at[p * PEERS + r], g_r.at[p * PEERS + r],
            at_peer((mine + r) % PEERS),
        )

    def send_gram(p):
        v = gacc[...]
        gall[p, mine] = jnp.where(
            glane[:32] < 64, v[:32], pltpu.roll(v[32:], 64, 1)
        )
        each(1, PEERS, lambda r: g_copy(p, r).start())

    def sum_gram(p):
        each(1, PEERS, lambda r: g_copy(p, r).wait_recv())
        v = jnp.sum(gall[p], axis=0)
        both_halves = jnp.concatenate([v, pltpu.roll(v, 64, 1)], axis=0)
        return jnp.where(glane < 64, both_halves, 0.0)

    def damping():
        m = sum_gram(0)

        def trace(v):
            return jnp.sum(jnp.where(glane == grow, v, 0.0), keepdims=True)

        m = m / jnp.maximum(trace(m), 1e-30)
        for _ in range(3):
            m = lax.dot_general(m[:, :PROBES], m, NN, precision=HIGHEST, preferred_element_type=F32)
            m = m / jnp.maximum(trace(m), 1e-30)
        diag = jnp.where(glane == grow, m, 0.0)
        top = jnp.max(diag, keepdims=True)
        ucol = jnp.sum(
            jnp.where(jnp.sum(diag, axis=0, keepdims=True) == top, jnp.where(glane < 64, m, 0.0), 0.0),
            axis=1, keepdims=True,
        )
        urow = jnp.sum(
            jnp.where(jnp.sum(diag, axis=1, keepdims=True) == top, m, 0.0), axis=0, keepdims=True
        )
        uu = jnp.maximum(jnp.sum(ucol * ucol, axis=0, keepdims=True), 1e-30)
        outer = ucol * (urow + pltpu.roll(urow, 64, 1)) / uu
        eye = jnp.where((glane == grow) | (glane - 64 == grow), 1.0, 0.0)
        t = eye - 0.875 * outer
        tinv[...] = eye + 7.0 * outer
        tmat[0:PROBES, :] = jnp.where(glane < 64, t, 0.0)
        tmat[PROBES:128, :] = jnp.where(glane >= 64, t, 0.0)

    def image_part(c, t):
        yo = (y + 1 + t) % NY
        return lax.dot_general(
            kmat[pl.ds(pl.multiple_of(yo * 2 * OWN, 2 * OWN), 2 * OWN), chunk_at(c)], st[...], NN,
            preferred_element_type=F32,
        )

    def merged(t, o):
        u = zacc[t, pl.ds(pl.multiple_of(o * OWN, OWN), OWN // 2), :]
        v = zacc[t, pl.ds(pl.multiple_of(o * OWN + OWN // 2, OWN // 2), OWN // 2), :]
        return jnp.where(wide < 64, u + pltpu.roll(u, 64, 1), v + pltpu.roll(v, 64, 1))

    def add_part(c, t):
        zacc[t] += image_part(c, t)

    def first_part(t):
        zacc[t] = image_part(0, t)

    def one_pass(c):
        take_chunk(c)
        add_gram(c)
        each(0, NY, lambda t: add_part(c, t))

    take_chunk(0)
    add_gram(0)
    send_gram(0)
    each(0, NY, first_part)
    each(1, CHUNKS - 1, one_pass)
    damping()
    take_chunk(CHUNKS - 1)
    add_gram(CHUNKS - 1)
    send_gram(1)

    def zc(t):
        return remote(zsend.at[t], zcrecv.at[t], zc_s.at[t], zc_r.at[t], at_peer(y * 2 + 1 - core))

    def zy(t):
        return remote(
            zout.at[t], zyrecv.at[t], zy_s.at[t], zy_r.at[t], at_peer(((y + 1 + t) % NY) * 2 + core)
        )

    def last_part(t):
        add_part(CHUNKS - 1, t)
        zsend[t] = merged(t, 1 - core)
        zc(t).start()

    def damped(t):
        zc(t).wait_recv()
        return lax.dot_general(
            merged(t, core) + zcrecv[t], tmat[...], NN, precision=HIGHEST, preferred_element_type=F32
        )

    def share(t):
        zout[t] = damped(t).astype(BF16)
        zy(t).start()

    each(0, NY, last_part)
    each(0, NY - 1, share)
    zmine[...] = damped(NY - 1)

    gram = sum_gram(1) / slab_total
    trace = jnp.sum(jnp.where(glane == grow, gram, 0.0), keepdims=True)
    m = jnp.where(glane < 64, gram, tinv[...])
    for k in range(0, PROBES, 8):
        cs, fs, rows = [], [], []
        for i in range(8):
            q = k + i
            c = jnp.broadcast_to(m[:, q : q + 1], (PROBES, 128))
            r = m[q : q + 1, :]
            for j in range(i):
                c = c - fs[j] * cs[j][q : q + 1, :]
                r = r - fs[j][q : q + 1, :] * rows[j]
            cs.append(c)
            fs.append(jnp.where(grow > q, c / c[q : q + 1, :], 0.0))
            rows.append(r)
        for f, r in zip(fs, rows):
            m = m - f * r
    d = jnp.sum(jnp.where(glane == grow, m, 0.0), axis=1, keepdims=True)
    upper = jnp.where(glane >= 64, m / jnp.sqrt(d), 0.0)
    lower = pltpu.roll(upper, 64, 1)

    own_lanes = pl.ds(pl.multiple_of((z // 2) * 128, 128), 128)
    stile = sfull[x, :, own_lanes]
    sown = jnp.where(z % 2 == 1, pltpu.roll(stile, 64, 1), stile)
    sdamp = lax.dot_general(
        tmat[0:PROBES, 0:PROBES], sown, NN, precision=HIGHEST, preferred_element_type=F32
    )
    basis = lax.dot_general(
        lower[:, :PROBES], sdamp, NN, precision=HIGHEST, preferred_element_type=F32
    )
    basis_ref[...] = basis[:, :BLK].astype(BF16)
    scale = jnp.sqrt(jnp.float32(PROBES * point_total) / trace) / slab_total

    each(1, NZ, lambda r: slab_z(r).wait_send())
    each(1, NX, lambda r: slab_x(r).wait_send())

    each(0, CHUNKS, lambda c: rs_all(c).wait_send())
    each(0, CHUNKS, lambda c: ag_all(c).wait_send())
    each(0, NY, lambda t: zc(t).wait_send())
    each(0, 2, lambda p: each(1, PEERS, lambda r: g_copy(p, r).wait_send()))
    each(0, NY - 1, lambda t: zy(t).wait())
    zs = zmine[...] + (zyrecv[0].astype(F32) + zyrecv[1].astype(F32) + zyrecv[2].astype(F32))
    for half, w in ((0, lower), (1, upper)):
        image_ref[:, half * 512 : half * 512 + 512] = scale * lax.dot_general(
            w, zs, NT, precision=HIGHEST, preferred_element_type=F32
        )


def finish_kernel(basis_in, image_in, basis_out, image_out):
    basis_out[...] = basis_in[...]
    image_out[...] = image_in[...]


def body(slab_points, col_points, probes):
    vmem = pl.BlockSpec(memory_space=pltpu.VMEM)
    hbm = pl.BlockSpec(memory_space=pl.ANY)
    dma = pltpu.SemaphoreType.DMA
    basis, image = pl.pallas_call(
        functools.partial(main_kernel, slab_total=A * PEERS, point_total=B * GROUP),
        out_shape=(
            jax.ShapeDtypeStruct((PROBES, BLK), BF16),
            jax.ShapeDtypeStruct((PROBES, OWN), F32),
        ),
        in_specs=[vmem, hbm, hbm],
        out_specs=(vmem, vmem),
        scratch_shapes=[
            pltpu.VMEM((DIMS, B), BF16),
            pltpu.VMEM((128, B), BF16),
            pltpu.VMEM((B, 256), BF16),
            pltpu.VMEM((NX, NZ, 32, 128), BF16),
            pltpu.VMEM((256, CA), BF16),
            pltpu.VMEM((B, A), BF16),
            pltpu.VMEM((CHUNKS, PROBES, CA), F32),
            pltpu.VMEM((CHUNKS, GROUP - 1, 8, 128), F32),
            pltpu.VMEM((CHUNKS, PROBES, CA), F32),
            pltpu.VMEM((CA, 128), BF16),
            pltpu.VMEM((NY, 2 * OWN, 128), F32),
            pltpu.VMEM((NY, OWN // 2, 128), F32),
            pltpu.VMEM((OWN // 2, 128), F32),
            pltpu.VMEM((NY, OWN // 2, 128), F32),
            pltpu.VMEM((NY - 1, OWN // 2, 128), BF16),
            pltpu.VMEM((NY - 1, OWN // 2, 128), BF16),
            pltpu.VMEM((PROBES, 128), F32),
            pltpu.VMEM((2, PEERS, 32, 128), F32),
            pltpu.VMEM((128, 128), F32),
            pltpu.VMEM((PROBES, 128), F32),
            dma((2,)),
            dma((NZ - 1,)), dma((NZ - 1,)), dma((NX - 1,)), dma((NX - 1,)),
            dma((CHUNKS,)), dma((CHUNKS,)), dma((CHUNKS,)), dma((CHUNKS,)),
            dma((NY,)), dma((NY,)), dma((NY - 1,)), dma((NY - 1,)),
            dma((2 * PEERS,)), dma((2 * PEERS,)),
        ],
        compiler_params=pltpu.CompilerParams(
            collective_id=0, has_side_effects=True, vmem_limit_bytes=62 << 20
        ),
        name="slab_kernel",
    )(slab_points, col_points, probes)
    return pl.pallas_call(
        finish_kernel,
        out_shape=(
            jax.ShapeDtypeStruct((PROBES, BLK), BF16),
            jax.ShapeDtypeStruct((PROBES, OWN), F32),
        ),
        in_specs=[vmem, vmem],
        out_specs=(vmem, vmem),
        name="finish",
    )(basis, image)


def solution(mesh):
    return jax.shard_map(
        body,
        mesh=mesh,
        in_specs=(P(None, ("row", "col")), P(None, "col"), P(None, "col")),
        out_specs=(P(None, ("row", "col")), P(None, ("col", "row"))),
        check_vma=False,
    )
```

```python
import functools
import math

import jax
import jax.numpy as jnp
from jax import lax
from jax.experimental import pallas as pl
from jax.experimental.pallas import tpu as pltpu
from jax.sharding import PartitionSpec as P

F32 = jnp.float32
BF16 = jnp.bfloat16
MESH = pl.DeviceIdType.MESH
NN = (((1,), (0,)), ((), ()))
NT = (((1,), (1,)), ((), ()))
LOG2E = 1.4426950408889634
HIGHEST = lax.Precision.HIGHEST

NX, NZ, NY, NCORE = 4, 8, 4, 2
GROUP = NX * NZ
PEERS = NY * NCORE
OTHERS = sorted(
    ((dx, dz) for dx in range(NX) for dz in range(NZ) if dx or dz),
    key=lambda o: (-min(o[0], NX - o[0]) - min(o[1], NZ - o[1]), o),
)
DIMS = 64
PROBES = 64
BLK = 64
CHUNKS = 4
CA = 512
A = CHUNKS * CA
B = 8192
TB = 4096
OWN = 1024


def split2(v):
    h = v.astype(BF16)
    return h, (v - h.astype(F32)).astype(BF16)


def dot3(a, b, dims):
    ah, al = split2(a)
    bh, bl = split2(b)

    def one(u, v):
        return lax.dot_general(u, v, dims, preferred_element_type=F32)

    return one(ah, bh) + (one(ah, bl) + one(al, bh))


def split3(v):
    h = v.astype(BF16).astype(F32)
    m = (v - h).astype(BF16).astype(F32)
    return h, m, v - h - m


def main_kernel(
    slab_ref, col_ref, probe_ref,
    basis_ref, image_ref,
    cols, probes, yt, xall, xaug, kmat, spart, rsrecv, sfull, st,
    zacc, zsend, zmine, zcrecv, zout, zyrecv, gacc, gall, tmat, tinv,
    in_sem, sz_s, sz_r, sx_s, sx_r, rs_s, rs_r, ag_s, ag_r,
    zc_s, zc_r, zy_s, zy_r, g_s, g_r,
    *, slab_total, point_total,
):
    row = lax.axis_index("row")
    col = lax.axis_index("col")
    core = lax.rem(row, 2)
    y = lax.rem(lax.div(row, 2), 4)
    zhi = lax.div(row, 8)
    z = zhi * 4 + lax.rem(col, 4)
    x = lax.div(col, 4)
    mine = y * NCORE + core

    def at_z(r):
        return at_offset(0, r)

    def at_x(r):
        return at_offset(r, 0)

    def at_offset(dx, dz):
        gx, gz = lax.rem(x + dx, NX), lax.rem(z + dz, NZ)
        return (lax.div(gz, 4) * 8 + mine, gx * 4 + lax.rem(gz, 4))

    def at_peer(q):
        return (zhi * 8 + q, col)

    def each(lo, hi, f):
        def step(r, _):
            f(r)
            return 0

        lax.fori_loop(lo, hi, step, 0)

    def unrolled(lo, hi, f):
        for r in range(lo, hi):
            f(r)

    def remote(src, dst, send, recv, device):
        return pltpu.make_async_remote_copy(
            src_ref=src, dst_ref=dst, send_sem=send, recv_sem=recv, device_id=device, device_id_type=MESH
        )

    cp_c = pltpu.make_async_copy(col_ref.at[:, pl.ds(pl.multiple_of(zhi * B, B), B)], cols, in_sem.at[0])
    cp_p = pltpu.make_async_copy(
        probe_ref.at[:, pl.ds(pl.multiple_of(zhi * B, B), B)], probes.at[pl.ds(0, PROBES), :], in_sem.at[1]
    )
    cp_c.start()
    cp_p.start()

    barrier = pltpu.get_barrier_semaphore()

    def greet(device):
        pl.semaphore_signal(barrier, inc=1, device_id=device, device_id_type=MESH)

    for dx, dz in OTHERS:
        greet(at_offset(dx, dz))
    unrolled(1, PEERS, lambda r: greet(at_peer(lax.rem(mine + r, PEERS))))

    s_in = slab_ref[...].astype(F32)
    xall[x, z] = jnp.concatenate([s_in[: DIMS // 2], s_in[DIMS // 2 :]], axis=1).astype(BF16)
    probes[PROBES:, :] = jnp.zeros((128 - PROBES, B), BF16)

    pl.semaphore_wait(barrier, GROUP - 1 + PEERS - 1)

    def slab_z(r):
        return remote(xall.at[x, z], xall.at[x, z], sz_s.at[r - 1], sz_r.at[r - 1], at_z(r))

    def slab_x(r):
        return remote(xall.at[x], xall.at[x], sx_s.at[r - 1], sx_r.at[r - 1], at_x(r))

    for r in (4, 3, 5, 2, 6, 1, 7):
        slab_z(r).start()

    cp_c.wait()
    alpha = LOG2E * 8.0 / DIMS

    def make_yt(i):
        b0 = pl.multiple_of(i * 512, 512)
        yv = cols[:, pl.ds(b0, 512)].astype(F32)
        yp = yv * (2.0 * alpha)
        h, m, l = split3(yp)
        nh, nm, nl = split3(-alpha * jnp.sum(yv * yv, axis=0, keepdims=True))
        r = lax.broadcasted_iota(jnp.int32, (DIMS, 512), 0)
        extra = jnp.where(
            r < 3, 1.0, jnp.where(r == 3, nh, jnp.where(r == 4, nm, jnp.where(r == 5, nl, 0.0)))
        )
        yt[pl.ds(b0, 512), 0:128] = jnp.transpose(jnp.concatenate([h, m], axis=0)).astype(BF16)
        yt[pl.ds(b0, 512), 128:256] = jnp.transpose(jnp.concatenate([l, extra], axis=0)).astype(BF16)

    each(0, B // 1024, make_yt)
    unrolled(1, NZ, lambda r: slab_z(r).wait_recv())
    for r in (2, 1, 3):
        slab_x(r).start()
    each(B // 1024, B // 512, make_yt)
    cp_p.wait()

    lane = lax.broadcasted_iota(jnp.int32, (DIMS // 2, 128), 1)

    def build_x(c):
        for pair in range(NZ // 2):
            va = xall[c, 2 * pair].astype(F32)
            vb = xall[c, 2 * pair + 1].astype(F32)
            even = jnp.where(lane < 64, va, pltpu.roll(vb, 64, 1))
            odd = jnp.where(lane < 64, pltpu.roll(va, 64, 1), vb)
            xv = jnp.concatenate([even, odd], axis=0)
            nh, nm, nl = split3(-alpha * jnp.sum(xv * xv, axis=0, keepdims=True))
            r = lax.broadcasted_iota(jnp.int32, (DIMS, 128), 0)
            extra = jnp.where(
                r == 0, nh,
                jnp.where(r == 1, nm, jnp.where(r == 2, nl, jnp.where(r < 6, 1.0, 0.0))),
            )
            whole = jnp.concatenate([xv, xv, xv, extra], axis=0).astype(BF16)
            xaug[:, pair * 128 : (pair + 1) * 128] = whole

    def piece(gx, gz):
        return (
            pl.ds(pl.multiple_of(gz * 8, 8), 8), pl.ds(pl.multiple_of(gx * 128, 128), 128)
        )

    def rs(c, k):
        dx, dz = OTHERS[k]
        there = piece(lax.rem(x + dx, NX), lax.rem(z + dz, NZ))
        return remote(
            spart.at[(c, *there)], rsrecv.at[c, k], rs_s.at[c], rs_r.at[c], at_offset(dx, dz)
        )

    def ag(c, k):
        here = sfull.at[(c, *piece(x, z))]
        return remote(here, here, ag_s.at[c], ag_r.at[c], at_offset(*OTHERS[k]))

    def to_others(f):
        for k in range(GROUP - 1):
            f(k)

    def rs_all(c):
        return remote(rsrecv.at[c], rsrecv.at[c], rs_s.at[c], rs_r.at[c], at_z(1))

    def ag_all(c):
        return remote(rsrecv.at[c], rsrecv.at[c], ag_s.at[c], ag_r.at[c], at_z(1))

    def reduce_own(c):
        rs_all(c).wait_recv()
        sfull[(c, *piece(x, z))] = spart[(c, *piece(x, z))] + jnp.sum(rsrecv[c], axis=0)
        to_others(lambda k: ag(c, k).start())

    def chunk_at(c):
        return pl.ds(pl.multiple_of(c * CA, CA), CA)

    def tile(c, i):
        b0 = pl.multiple_of(i * TB, TB)
        t = lax.dot_general(yt[pl.ds(b0, TB), :], xaug[...], NN, preferred_element_type=F32)
        k = jnp.exp2(t).astype(BF16)
        kmat[pl.ds(b0, TB), chunk_at(c)] = k
        return lax.dot_general(probes[:, pl.ds(b0, TB)], k, NN, preferred_element_type=F32)[:PROBES]

    def clear_part(c):
        spart[c] = jnp.zeros((PROBES, CA), F32)

    each(0, CHUNKS, clear_part)

    def phase1(n):
        index = jnp.where(n == 0, 2 * x, jnp.where(n <= 2 * x, n - 1, n))
        c = index // 2
        half = index % 2

        @pl.when((half == 0) & (c != x))
        def _():
            slab_x((x - c + NX) % NX).wait_recv()

        build_x(c)
        spart[c] += tile(c, half)
        pl.when(half == 1)(lambda: to_others(lambda k: rs(c, k).start()))
        pl.when(n == 6)(lambda: reduce_own(0))

    each(0, 2 * CHUNKS, phase1)
    reduce_own(1)
    reduce_own(2)

    wide = lax.broadcasted_iota(jnp.int32, (OWN // 2, 128), 1)
    glane = lax.broadcasted_iota(jnp.int32, (PROBES, 128), 1)
    grow = lax.broadcasted_iota(jnp.int32, (PROBES, 128), 0)
    gacc[...] = jnp.zeros((PROBES, 128), F32)

    def take_chunk(c):
        s = sfull[c]
        hi = s.astype(BF16).astype(F32)
        st[...] = jnp.transpose(jnp.concatenate([hi, s - hi], axis=0)).astype(BF16)

    def add_gram(c):
        s = sfull[c]
        gacc[:, 0:PROBES] += lax.dot_general(s, s, NT, precision=HIGHEST, preferred_element_type=F32)

    def g_copy(p, r):
        return remote(
            gall.at[p, mine], gall.at[p, mine], g_s.at[p * PEERS + r], g_r.at[p * PEERS + r],
            at_peer(lax.rem(mine + r, PEERS)),
        )

    def send_gram(p):
        v = gacc[...]
        gall[p, mine] = jnp.where(
            glane[:32] < 64, v[:32], pltpu.roll(v[32:], 64, 1)
        )
        unrolled(1, PEERS, lambda r: g_copy(p, r).start())

    def sum_gram(p):
        unrolled(1, PEERS, lambda r: g_copy(p, r).wait_recv())
        v = jnp.sum(gall[p], axis=0)
        both_halves = jnp.concatenate([v, pltpu.roll(v, 64, 1)], axis=0)
        return jnp.where(glane < 64, both_halves, 0.0)

    def damping():
        m = sum_gram(0)

        def trace(v):
            return jnp.sum(jnp.where(glane == grow, v, 0.0), keepdims=True)

        m = m / jnp.maximum(trace(m), 1e-30)
        for _ in range(3):
            m = lax.dot_general(m[:, :PROBES], m, NN, precision=HIGHEST, preferred_element_type=F32)
            m = m / jnp.maximum(trace(m), 1e-30)
        diag = jnp.where(glane == grow, m, 0.0)
        top = jnp.max(diag, keepdims=True)
        ucol = jnp.sum(
            jnp.where(jnp.sum(diag, axis=0, keepdims=True) == top, jnp.where(glane < 64, m, 0.0), 0.0),
            axis=1, keepdims=True,
        )
        urow = jnp.sum(
            jnp.where(jnp.sum(diag, axis=1, keepdims=True) == top, m, 0.0), axis=0, keepdims=True
        )
        uu = jnp.maximum(jnp.sum(ucol * ucol, axis=0, keepdims=True), 1e-30)
        outer = ucol * (urow + pltpu.roll(urow, 64, 1)) / uu
        eye = jnp.where((glane == grow) | (glane - 64 == grow), 1.0, 0.0)
        t = eye - 0.875 * outer
        tinv[...] = eye + 7.0 * outer
        tmat[0:PROBES, :] = jnp.where(glane < 64, t, 0.0)
        tmat[PROBES:128, :] = jnp.where(glane >= 64, t, 0.0)

    def image_part(c, t):
        yo = lax.rem(y + 1 + t, NY)
        return lax.dot_general(
            kmat[pl.ds(pl.multiple_of(yo * 2 * OWN, 2 * OWN), 2 * OWN), chunk_at(c)], st[...], NN,
            preferred_element_type=F32,
        )

    def merged(t, o):
        u = zacc[t, pl.ds(pl.multiple_of(o * OWN, OWN), OWN // 2), :]
        v = zacc[t, pl.ds(pl.multiple_of(o * OWN + OWN // 2, OWN // 2), OWN // 2), :]
        return jnp.where(wide < 64, u + pltpu.roll(u, 64, 1), v + pltpu.roll(v, 64, 1))

    def add_part(c, t):
        zacc[t] += image_part(c, t)

    def first_part(t):
        zacc[t] = image_part(0, t)

    def one_pass(c):
        ag_all(c).wait_recv()
        take_chunk(c)
        add_gram(c)
        each(0, NY, lambda t: add_part(c, t))

    ag_all(0).wait_recv()
    take_chunk(0)
    add_gram(0)
    send_gram(0)
    each(0, NY, first_part)
    reduce_own(3)
    each(1, CHUNKS - 1, one_pass)
    damping()
    ag_all(CHUNKS - 1).wait_recv()
    add_gram(CHUNKS - 1)
    send_gram(1)
    take_chunk(CHUNKS - 1)

    def zc(t):
        return remote(zsend.at[t], zcrecv.at[t], zc_s.at[t], zc_r.at[t], at_peer(y * 2 + 1 - core))

    def zy(t):
        return remote(
            zout.at[t], zyrecv.at[t], zy_s.at[t], zy_r.at[t], at_peer((lax.rem(y + 1 + t, NY)) * 2 + core)
        )

    def last_part(t):
        add_part(CHUNKS - 1, t)
        zsend[t] = merged(t, 1 - core)
        zc(t).start()

    def damped(t):
        zc(t).wait_recv()
        return dot3(merged(t, core) + zcrecv[t], tmat[...], NN)

    def share(t):
        zout[t] = damped(t).astype(BF16)
        zy(t).start()

    each(0, NY, last_part)
    each(0, NY - 1, share)
    zmine[...] = damped(NY - 1)

    own_lanes = pl.ds(pl.multiple_of((z // 2) * 128, 128), 128)
    stile = sfull[x, :, own_lanes]
    sown = jnp.where(z % 2 == 1, pltpu.roll(stile, 64, 1), stile)
    sdamp = lax.dot_general(
        tmat[0:PROBES, 0:PROBES], sown, NN, precision=HIGHEST, preferred_element_type=F32
    )
    gram = sum_gram(1) / slab_total
    trace = jnp.sum(jnp.where(glane == grow, gram, 0.0), keepdims=True)
    m = jnp.where(glane < 64, gram, tinv[...])
    for k in range(0, PROBES, 8):
        cs, fs, rows = [], [], []
        for i in range(8):
            q = k + i
            c = jnp.broadcast_to(m[:, q : q + 1], (PROBES, 128))
            r = m[q : q + 1, :]
            for j in range(i):
                c = c - fs[j] * cs[j][q : q + 1, :]
                r = r - fs[j][q : q + 1, :] * rows[j]
            cs.append(c)
            fs.append(jnp.where(grow > q, c / c[q : q + 1, :], 0.0))
            rows.append(r)
        for f, r in zip(fs, rows):
            m = m - f * r
    d = jnp.sum(jnp.where(glane == grow, m, 0.0), axis=1, keepdims=True)
    upper = jnp.where(glane >= 64, m / jnp.sqrt(d), 0.0)
    lower = pltpu.roll(upper, 64, 1)

    basis = lax.dot_general(
        lower[:, :PROBES], sdamp, NN, precision=HIGHEST, preferred_element_type=F32
    )
    basis_ref[...] = basis[:, :BLK].astype(BF16)
    scale = jnp.sqrt(jnp.float32(PROBES * point_total) / trace) / slab_total

    each(1, NZ, lambda r: slab_z(r).wait_send())
    each(1, NX, lambda r: slab_x(r).wait_send())

    each(0, CHUNKS, lambda c: rs_all(c).wait_send())
    each(0, CHUNKS, lambda c: ag_all(c).wait_send())
    each(0, NY, lambda t: zc(t).wait_send())
    each(0, 2, lambda p: each(1, PEERS, lambda r: g_copy(p, r).wait_send()))
    each(0, NY - 1, lambda t: zy(t).wait())
    zs = zmine[...] + (zyrecv[0].astype(F32) + zyrecv[1].astype(F32) + zyrecv[2].astype(F32))
    halves = scale * dot3(jnp.concatenate([lower, upper], axis=0), zs, NT)
    image_ref[:, : OWN // 2] = halves[:PROBES]
    image_ref[:, OWN // 2 :] = halves[PROBES:]


def finish_kernel(basis_in, image_in, basis_out, image_out):
    basis_out[...] = basis_in[...]
    image_out[...] = image_in[...]


def body(slab_points, col_points, probes):
    vmem = pl.BlockSpec(memory_space=pltpu.VMEM)
    hbm = pl.BlockSpec(memory_space=pl.ANY)
    dma = pltpu.SemaphoreType.DMA
    basis, image = pl.pallas_call(
        functools.partial(main_kernel, slab_total=A * PEERS, point_total=B * GROUP),
        out_shape=(
            jax.ShapeDtypeStruct((PROBES, BLK), BF16),
            jax.ShapeDtypeStruct((PROBES, OWN), F32),
        ),
        in_specs=[vmem, hbm, hbm],
        out_specs=(vmem, vmem),
        scratch_shapes=[
            pltpu.VMEM((DIMS, B), BF16),
            pltpu.VMEM((128, B), BF16),
            pltpu.VMEM((B, 256), BF16),
            pltpu.VMEM((NX, NZ, 32, 128), BF16),
            pltpu.VMEM((256, CA), BF16),
            pltpu.VMEM((B, A), BF16),
            pltpu.VMEM((CHUNKS, PROBES, CA), F32),
            pltpu.VMEM((CHUNKS, GROUP - 1, 8, 128), F32),
            pltpu.VMEM((CHUNKS, PROBES, CA), F32),
            pltpu.VMEM((CA, 128), BF16),
            pltpu.VMEM((NY, 2 * OWN, 128), F32),
            pltpu.VMEM((NY, OWN // 2, 128), F32),
            pltpu.VMEM((OWN // 2, 128), F32),
            pltpu.VMEM((NY, OWN // 2, 128), F32),
            pltpu.VMEM((NY - 1, OWN // 2, 128), BF16),
            pltpu.VMEM((NY - 1, OWN // 2, 128), BF16),
            pltpu.VMEM((PROBES, 128), F32),
            pltpu.VMEM((2, PEERS, 32, 128), F32),
            pltpu.VMEM((128, 128), F32),
            pltpu.VMEM((PROBES, 128), F32),
            dma((2,)),
            dma((NZ - 1,)), dma((NZ - 1,)), dma((NX - 1,)), dma((NX - 1,)),
            dma((CHUNKS,)), dma((CHUNKS,)), dma((CHUNKS,)), dma((CHUNKS,)),
            dma((NY,)), dma((NY,)), dma((NY - 1,)), dma((NY - 1,)),
            dma((2 * PEERS,)), dma((2 * PEERS,)),
        ],
        compiler_params=pltpu.CompilerParams(
            collective_id=0, has_side_effects=True, vmem_limit_bytes=62 << 20
        ),
        name="slab_kernel",
    )(slab_points, col_points, probes)
    return pl.pallas_call(
        finish_kernel,
        out_shape=(
            jax.ShapeDtypeStruct((PROBES, BLK), BF16),
            jax.ShapeDtypeStruct((PROBES, OWN), F32),
        ),
        in_specs=[vmem, vmem],
        out_specs=(vmem, vmem),
        name="finish",
    )(basis, image)


def solution(mesh):
    return jax.shard_map(
        body,
        mesh=mesh,
        in_specs=(P(None, ("row", "col")), P(None, "col"), P(None, "col")),
        out_specs=(P(None, ("row", "col")), P(None, ("col", "row"))),
        check_vma=False,
    )
```

```python
import functools
import math

import jax
import jax.numpy as jnp
from jax import lax
from jax.experimental import pallas as pl
from jax.experimental.pallas import tpu as pltpu
from jax.sharding import PartitionSpec as P

F32 = jnp.float32
BF16 = jnp.bfloat16
MESH = pl.DeviceIdType.MESH
NN = (((1,), (0,)), ((), ()))
NT = (((1,), (1,)), ((), ()))
LOG2E = 1.4426950408889634
HIGHEST = lax.Precision.HIGHEST

NX, NZ, NY, NCORE = 4, 8, 4, 2
GROUP = NX * NZ
PEERS = NY * NCORE
OTHERS = sorted(
    ((dx, dz) for dx in range(NX) for dz in range(NZ) if dx or dz),
    key=lambda o: (-min(o[0], NX - o[0]) - min(o[1], NZ - o[1]), o),
)
DIMS = 64
PROBES = 64
BLK = 64
CHUNKS = 4
CA = 512
A = CHUNKS * CA
B = 8192
TB = 4096
OWN = 1024


def split2(v):
    h = v.astype(BF16)
    return h, (v - h.astype(F32)).astype(BF16)


def dot3(a, b, dims):
    ah, al = split2(a)
    bh, bl = split2(b)

    def one(u, v):
        return lax.dot_general(u, v, dims, preferred_element_type=F32)

    return one(ah, bh) + (one(ah, bl) + one(al, bh))


def split3(v):
    h = v.astype(BF16).astype(F32)
    m = (v - h).astype(BF16).astype(F32)
    return h, m, v - h - m


def main_kernel(
    slab_ref, col_ref, probe_ref,
    basis_ref, image_ref,
    cols, probes, yt, xall, xaug, kmat, spart, rsrecv, sfull, st,
    zacc, zsend, zmine, zcrecv, zout, zyrecv, gacc, gall, tmat, tinv,
    in_sem, sz_s, sz_r, sx_s, sx_r, rs_s, rs_r, az_s, az_r, ax_s, ax_r,
    zc_s, zc_r, zy_s, zy_r, g_s, g_r,
    *, slab_total, point_total,
):
    row = lax.axis_index("row")
    col = lax.axis_index("col")
    core = lax.rem(row, 2)
    y = lax.rem(lax.div(row, 2), 4)
    zhi = lax.div(row, 8)
    z = zhi * 4 + lax.rem(col, 4)
    x = lax.div(col, 4)
    mine = y * NCORE + core

    def at_z(r):
        return at_offset(0, r)

    def at_x(r):
        return at_offset(r, 0)

    def at_offset(dx, dz):
        gx, gz = lax.rem(x + dx, NX), lax.rem(z + dz, NZ)
        return (lax.div(gz, 4) * 8 + mine, gx * 4 + lax.rem(gz, 4))

    def at_peer(q):
        return (zhi * 8 + q, col)

    def each(lo, hi, f):
        def step(r, _):
            f(r)
            return 0

        lax.fori_loop(lo, hi, step, 0)

    def unrolled(lo, hi, f):
        for r in range(lo, hi):
            f(r)

    def remote(src, dst, send, recv, device):
        return pltpu.make_async_remote_copy(
            src_ref=src, dst_ref=dst, send_sem=send, recv_sem=recv, device_id=device, device_id_type=MESH
        )

    cp_c = pltpu.make_async_copy(col_ref.at[:, pl.ds(pl.multiple_of(zhi * B, B), B)], cols, in_sem.at[0])
    cp_p = pltpu.make_async_copy(
        probe_ref.at[:, pl.ds(pl.multiple_of(zhi * B, B), B)], probes.at[pl.ds(0, PROBES), :], in_sem.at[1]
    )
    cp_c.start()
    cp_p.start()

    barrier = pltpu.get_barrier_semaphore()

    def greet(device):
        pl.semaphore_signal(barrier, inc=1, device_id=device, device_id_type=MESH)

    for dx, dz in OTHERS:
        greet(at_offset(dx, dz))
    unrolled(1, PEERS, lambda r: greet(at_peer(lax.rem(mine + r, PEERS))))

    s_in = slab_ref[...].astype(F32)
    xall[x, z] = jnp.concatenate([s_in[: DIMS // 2], s_in[DIMS // 2 :]], axis=1).astype(BF16)
    probes[PROBES:, :] = jnp.zeros((128 - PROBES, B), BF16)

    pl.semaphore_wait(barrier, GROUP - 1 + PEERS - 1)

    def slab_z(r):
        return remote(xall.at[x, z], xall.at[x, z], sz_s.at[r - 1], sz_r.at[r - 1], at_z(r))

    def slab_x(r):
        return remote(xall.at[x], xall.at[x], sx_s.at[r - 1], sx_r.at[r - 1], at_x(r))

    for r in (4, 3, 5, 2, 6, 1, 7):
        slab_z(r).start()

    cp_c.wait()
    alpha = LOG2E * 8.0 / DIMS

    def make_yt(i):
        b0 = pl.multiple_of(i * 512, 512)
        yv = cols[:, pl.ds(b0, 512)].astype(F32)
        yp = yv * (2.0 * alpha)
        h, m, l = split3(yp)
        nh, nm, nl = split3(-alpha * jnp.sum(yv * yv, axis=0, keepdims=True))
        r = lax.broadcasted_iota(jnp.int32, (DIMS, 512), 0)
        extra = jnp.where(
            r < 3, 1.0, jnp.where(r == 3, nh, jnp.where(r == 4, nm, jnp.where(r == 5, nl, 0.0)))
        )
        yt[pl.ds(b0, 512), 0:128] = jnp.transpose(jnp.concatenate([h, m], axis=0)).astype(BF16)
        yt[pl.ds(b0, 512), 128:256] = jnp.transpose(jnp.concatenate([l, extra], axis=0)).astype(BF16)

    each(0, B // 1024, make_yt)
    unrolled(1, NZ, lambda r: slab_z(r).wait_recv())
    for r in (2, 1, 3):
        slab_x(r).start()
    each(B // 1024, B // 512, make_yt)
    cp_p.wait()

    lane = lax.broadcasted_iota(jnp.int32, (DIMS // 2, 128), 1)

    def build_x(c):
        for pair in range(NZ // 2):
            va = xall[c, 2 * pair].astype(F32)
            vb = xall[c, 2 * pair + 1].astype(F32)
            even = jnp.where(lane < 64, va, pltpu.roll(vb, 64, 1))
            odd = jnp.where(lane < 64, pltpu.roll(va, 64, 1), vb)
            xv = jnp.concatenate([even, odd], axis=0)
            nh, nm, nl = split3(-alpha * jnp.sum(xv * xv, axis=0, keepdims=True))
            r = lax.broadcasted_iota(jnp.int32, (DIMS, 128), 0)
            extra = jnp.where(
                r == 0, nh,
                jnp.where(r == 1, nm, jnp.where(r == 2, nl, jnp.where(r < 6, 1.0, 0.0))),
            )
            whole = jnp.concatenate([xv, xv, xv, extra], axis=0).astype(BF16)
            xaug[:, pair * 128 : (pair + 1) * 128] = whole

    def piece(gx, gz):
        return (
            pl.ds(pl.multiple_of(gz * 8, 8), 8), pl.ds(pl.multiple_of(gx * 128, 128), 128)
        )

    def rs(c, k):
        dx, dz = OTHERS[k]
        there = piece(lax.rem(x + dx, NX), lax.rem(z + dz, NZ))
        return remote(
            spart.at[(c, *there)], rsrecv.at[c, k], rs_s.at[c], rs_r.at[c], at_offset(dx, dz)
        )

    def to_others(f):
        for k in range(GROUP - 1):
            f(k)

    def rs_all(c):
        return remote(rsrecv.at[c], rsrecv.at[c], rs_s.at[c], rs_r.at[c], at_z(1))

    def az(c, r):
        here = sfull.at[(c, *piece(x, z))]
        return remote(here, here, az_s.at[c], az_r.at[c], at_z(r))

    def ax(c, r):
        here = sfull.at[c, :, pl.ds(pl.multiple_of(x * 128, 128), 128)]
        return remote(here, here, ax_s.at[c], ax_r.at[c], at_x(r))

    def az_all(c):
        some = rsrecv.at[c, pl.ds(0, NZ - 1)]
        return remote(some, some, az_s.at[c], az_r.at[c], at_z(1))

    def ax_all(c):
        some = rsrecv.at[c, pl.ds(0, (NX - 1) * NZ)]
        return remote(some, some, ax_s.at[c], ax_r.at[c], at_z(1))

    def sum_own(c):
        rs_all(c).wait_recv()
        sfull[(c, *piece(x, z))] = spart[(c, *piece(x, z))] + jnp.sum(rsrecv[c], axis=0)

    def reduce_own(c):
        sum_own(c)
        unrolled(1, NZ, lambda r: az(c, r).start())

    def gather_x(c):
        az_all(c).wait_recv()
        unrolled(1, NX, lambda r: ax(c, r).start())

    def chunk_at(c):
        return pl.ds(pl.multiple_of(c * CA, CA), CA)

    def tile(c, i):
        b0 = pl.multiple_of(i * TB, TB)
        t = lax.dot_general(yt[pl.ds(b0, TB), :], xaug[...], NN, preferred_element_type=F32)
        k = jnp.exp2(t).astype(BF16)
        kmat[pl.ds(b0, TB), chunk_at(c)] = k
        return lax.dot_general(probes[:, pl.ds(b0, TB)], k, NN, preferred_element_type=F32)[:PROBES]

    def clear_part(c):
        spart[c] = jnp.zeros((PROBES, CA), F32)

    each(0, CHUNKS, clear_part)

    def phase1(n):
        index = jnp.where(n == 0, 2 * x, jnp.where(n <= 2 * x, n - 1, n))
        c = index // 2
        half = index % 2

        @pl.when((half == 0) & (c != x))
        def _():
            slab_x((x - c + NX) % NX).wait_recv()

        pl.when((half == 0) | (c == x))(lambda: build_x(c))
        spart[c] += tile(c, half)
        pl.when(half == 1)(lambda: to_others(lambda k: rs(c, k).start()))
        pl.when(n == 6)(lambda: reduce_own(0))

    each(0, 2 * CHUNKS, phase1)
    reduce_own(1)
    gather_x(0)
    reduce_own(2)
    gather_x(1)

    wide = lax.broadcasted_iota(jnp.int32, (OWN // 2, 128), 1)
    glane = lax.broadcasted_iota(jnp.int32, (PROBES, 128), 1)
    grow = lax.broadcasted_iota(jnp.int32, (PROBES, 128), 0)
    gacc[...] = jnp.zeros((PROBES, 128), F32)

    def take_chunk(c):
        s = sfull[c]
        hi = s.astype(BF16).astype(F32)
        st[...] = jnp.transpose(jnp.concatenate([hi, s - hi], axis=0)).astype(BF16)

    def add_gram(c):
        s = sfull[c]
        gacc[:, 0:PROBES] += lax.dot_general(s, s, NT, precision=HIGHEST, preferred_element_type=F32)

    def g_copy(p, r):
        return remote(
            gall.at[p, mine], gall.at[p, mine], g_s.at[p * PEERS + r], g_r.at[p * PEERS + r],
            at_peer(lax.rem(mine + r, PEERS)),
        )

    def send_gram(p):
        v = gacc[...]
        gall[p, mine] = jnp.where(
            glane[:32] < 64, v[:32], pltpu.roll(v[32:], 64, 1)
        )
        unrolled(1, PEERS, lambda r: g_copy(p, r).start())

    def sum_gram(p):
        unrolled(1, PEERS, lambda r: g_copy(p, r).wait_recv())
        v = jnp.sum(gall[p], axis=0)
        both_halves = jnp.concatenate([v, pltpu.roll(v, 64, 1)], axis=0)
        return jnp.where(glane < 64, both_halves, 0.0)

    def damping():
        m = sum_gram(0)

        def trace(v):
            return jnp.sum(jnp.where(glane == grow, v, 0.0), keepdims=True)

        m = m / jnp.maximum(trace(m), 1e-30)
        for _ in range(3):
            m = lax.dot_general(m[:, :PROBES], m, NN, precision=HIGHEST, preferred_element_type=F32)
            m = m / jnp.maximum(trace(m), 1e-30)
        diag = jnp.where(glane == grow, m, 0.0)
        top = jnp.max(diag, keepdims=True)
        ucol = jnp.sum(
            jnp.where(jnp.sum(diag, axis=0, keepdims=True) == top, jnp.where(glane < 64, m, 0.0), 0.0),
            axis=1, keepdims=True,
        )
        urow = jnp.sum(
            jnp.where(jnp.sum(diag, axis=1, keepdims=True) == top, m, 0.0), axis=0, keepdims=True
        )
        uu = jnp.maximum(jnp.sum(ucol * ucol, axis=0, keepdims=True), 1e-30)
        outer = ucol * (urow + pltpu.roll(urow, 64, 1)) / uu
        eye = jnp.where((glane == grow) | (glane - 64 == grow), 1.0, 0.0)
        t = eye - 0.875 * outer
        tinv[...] = eye + 7.0 * outer
        tmat[0:PROBES, :] = jnp.where(glane < 64, t, 0.0)
        tmat[PROBES:128, :] = jnp.where(glane >= 64, t, 0.0)

    def image_part(c, t):
        yo = lax.rem(y + 1 + t, NY)
        return lax.dot_general(
            kmat[pl.ds(pl.multiple_of(yo * 2 * OWN, 2 * OWN), 2 * OWN), chunk_at(c)], st[...], NN,
            preferred_element_type=F32,
        )

    def merged(t, o):
        u = zacc[t, pl.ds(pl.multiple_of(o * OWN, OWN), OWN // 2), :]
        v = zacc[t, pl.ds(pl.multiple_of(o * OWN + OWN // 2, OWN // 2), OWN // 2), :]
        return jnp.where(wide < 64, u + pltpu.roll(u, 64, 1), v + pltpu.roll(v, 64, 1))

    def add_part(c, t):
        zacc[t] += image_part(c, t)

    def first_part(t):
        zacc[t] = image_part(0, t)

    def one_pass(c):
        ax_all(c).wait_recv()
        take_chunk(c)
        add_gram(c)
        each(0, NY, lambda t: add_part(c, t))

    reduce_own(3)
    gather_x(2)
    ax_all(0).wait_recv()
    take_chunk(0)
    add_gram(0)
    send_gram(0)
    each(0, NY, first_part)
    one_pass(1)
    gather_x(3)
    one_pass(2)
    damping()
    ax_all(CHUNKS - 1).wait_recv()
    add_gram(CHUNKS - 1)
    send_gram(1)
    take_chunk(CHUNKS - 1)

    def zc(t):
        return remote(zsend.at[t], zcrecv.at[t], zc_s.at[t], zc_r.at[t], at_peer(y * 2 + 1 - core))

    def zy(t):
        return remote(
            zout.at[t], zyrecv.at[t], zy_s.at[t], zy_r.at[t], at_peer((lax.rem(y + 1 + t, NY)) * 2 + core)
        )

    def last_part(t):
        add_part(CHUNKS - 1, t)
        zsend[t] = merged(t, 1 - core)
        zc(t).start()

    def damped(t):
        zc(t).wait_recv()
        return dot3(merged(t, core) + zcrecv[t], tmat[...], NN)

    def share(t):
        zout[t] = damped(t).astype(BF16)
        zy(t).start()

    each(0, NY, last_part)
    each(0, NY - 1, share)
    zmine[...] = damped(NY - 1)

    own_lanes = pl.ds(pl.multiple_of((z // 2) * 128, 128), 128)
    stile = sfull[x, :, own_lanes]
    sown = jnp.where(z % 2 == 1, pltpu.roll(stile, 64, 1), stile)
    sdamp = lax.dot_general(
        tmat[0:PROBES, 0:PROBES], sown, NN, precision=HIGHEST, preferred_element_type=F32
    )
    gram = sum_gram(1) / slab_total
    trace = jnp.sum(jnp.where(glane == grow, gram, 0.0), keepdims=True)
    m = jnp.where(glane < 64, gram, tinv[...])
    for k in range(0, PROBES, 8):
        cs, fs, rows = [], [], []
        for i in range(8):
            q = k + i
            c = jnp.broadcast_to(m[:, q : q + 1], (PROBES, 128))
            r = m[q : q + 1, :]
            for j in range(i):
                c = c - fs[j] * cs[j][q : q + 1, :]
                r = r - fs[j][q : q + 1, :] * rows[j]
            cs.append(c)
            fs.append(jnp.where(grow > q, c / c[q : q + 1, :], 0.0))
            rows.append(r)
        for f, r in zip(fs, rows):
            m = m - f * r
    d = jnp.sum(jnp.where(glane == grow, m, 0.0), axis=1, keepdims=True)
    upper = jnp.where(glane >= 64, m / jnp.sqrt(d), 0.0)
    lower = pltpu.roll(upper, 64, 1)

    basis = lax.dot_general(
        lower[:, :PROBES], sdamp, NN, precision=HIGHEST, preferred_element_type=F32
    )
    basis_ref[...] = basis[:, :BLK].astype(BF16)
    scale = jnp.sqrt(jnp.float32(PROBES * point_total) / trace) / slab_total

    each(1, NZ, lambda r: slab_z(r).wait_send())
    each(1, NX, lambda r: slab_x(r).wait_send())

    each(0, CHUNKS, lambda c: rs_all(c).wait_send())
    each(0, CHUNKS, lambda c: az_all(c).wait_send())
    each(0, CHUNKS, lambda c: ax_all(c).wait_send())
    each(0, NY, lambda t: zc(t).wait_send())
    each(0, 2, lambda p: each(1, PEERS, lambda r: g_copy(p, r).wait_send()))
    each(0, NY - 1, lambda t: zy(t).wait())
    zs = zmine[...] + (zyrecv[0].astype(F32) + zyrecv[1].astype(F32) + zyrecv[2].astype(F32))
    halves = scale * dot3(jnp.concatenate([lower, upper], axis=0), zs, NT)
    image_ref[:, : OWN // 2] = halves[:PROBES]
    image_ref[:, OWN // 2 :] = halves[PROBES:]


def finish_kernel(basis_in, image_in, basis_out, image_out):
    basis_out[...] = basis_in[...]
    image_out[...] = image_in[...]


def body(slab_points, col_points, probes):
    vmem = pl.BlockSpec(memory_space=pltpu.VMEM)
    hbm = pl.BlockSpec(memory_space=pl.ANY)
    dma = pltpu.SemaphoreType.DMA
    basis, image = pl.pallas_call(
        functools.partial(main_kernel, slab_total=A * PEERS, point_total=B * GROUP),
        out_shape=(
            jax.ShapeDtypeStruct((PROBES, BLK), BF16),
            jax.ShapeDtypeStruct((PROBES, OWN), F32),
        ),
        in_specs=[vmem, hbm, hbm],
        out_specs=(vmem, vmem),
        scratch_shapes=[
            pltpu.VMEM((DIMS, B), BF16),
            pltpu.VMEM((128, B), BF16),
            pltpu.VMEM((B, 256), BF16),
            pltpu.VMEM((NX, NZ, 32, 128), BF16),
            pltpu.VMEM((256, CA), BF16),
            pltpu.VMEM((B, A), BF16),
            pltpu.VMEM((CHUNKS, PROBES, CA), F32),
            pltpu.VMEM((CHUNKS, GROUP - 1, 8, 128), F32),
            pltpu.VMEM((CHUNKS, PROBES, CA), F32),
            pltpu.VMEM((CA, 128), BF16),
            pltpu.VMEM((NY, 2 * OWN, 128), F32),
            pltpu.VMEM((NY, OWN // 2, 128), F32),
            pltpu.VMEM((OWN // 2, 128), F32),
            pltpu.VMEM((NY, OWN // 2, 128), F32),
            pltpu.VMEM((NY - 1, OWN // 2, 128), BF16),
            pltpu.VMEM((NY - 1, OWN // 2, 128), BF16),
            pltpu.VMEM((PROBES, 128), F32),
            pltpu.VMEM((2, PEERS, 32, 128), F32),
            pltpu.VMEM((128, 128), F32),
            pltpu.VMEM((PROBES, 128), F32),
            dma((2,)),
            dma((NZ - 1,)), dma((NZ - 1,)), dma((NX - 1,)), dma((NX - 1,)),
            dma((CHUNKS,)), dma((CHUNKS,)), dma((CHUNKS,)), dma((CHUNKS,)), dma((CHUNKS,)), dma((CHUNKS,)),
            dma((NY,)), dma((NY,)), dma((NY - 1,)), dma((NY - 1,)),
            dma((2 * PEERS,)), dma((2 * PEERS,)),
        ],
        compiler_params=pltpu.CompilerParams(
            collective_id=0, has_side_effects=True, vmem_limit_bytes=62 << 20
        ),
        name="slab_kernel",
    )(slab_points, col_points, probes)
    return pl.pallas_call(
        finish_kernel,
        out_shape=(
            jax.ShapeDtypeStruct((PROBES, BLK), BF16),
            jax.ShapeDtypeStruct((PROBES, OWN), F32),
        ),
        in_specs=[vmem, vmem],
        out_specs=(vmem, vmem),
        name="finish",
    )(basis, image)


def solution(mesh):
    return jax.shard_map(
        body,
        mesh=mesh,
        in_specs=(P(None, ("row", "col")), P(None, "col"), P(None, "col")),
        out_specs=(P(None, ("row", "col")), P(None, ("col", "row"))),
        check_vma=False,
    )
```

```python
import functools
import math

import jax
import jax.numpy as jnp
from jax import lax
from jax.experimental import pallas as pl
from jax.experimental.pallas import tpu as pltpu
from jax.sharding import PartitionSpec as P

F32 = jnp.float32
BF16 = jnp.bfloat16
MESH = pl.DeviceIdType.MESH
NN = (((1,), (0,)), ((), ()))
NT = (((1,), (1,)), ((), ()))
LOG2E = 1.4426950408889634
HIGHEST = lax.Precision.HIGHEST

NX, NZ, NY, NCORE = 4, 8, 4, 2
GROUP = NX * NZ
PEERS = NY * NCORE
OTHERS = sorted(
    ((dx, dz) for dx in range(NX) for dz in range(NZ) if dx or dz),
    key=lambda o: (-min(o[0], NX - o[0]) - min(o[1], NZ - o[1]), o),
)
DIMS = 64
PROBES = 64
BLK = 64
CHUNKS = 4
CA = 512
A = CHUNKS * CA
B = 8192
TB = 4096
OWN = 1024


def split2(v):
    h = v.astype(BF16)
    return h, (v - h.astype(F32)).astype(BF16)


def dot3(a, b, dims):
    ah, al = split2(a)
    bh, bl = split2(b)

    def one(u, v):
        return lax.dot_general(u, v, dims, preferred_element_type=F32)

    return one(ah, bh) + (one(ah, bl) + one(al, bh))


def split3(v):
    h = v.astype(BF16).astype(F32)
    m = (v - h).astype(BF16).astype(F32)
    return h, m, v - h - m


def main_kernel(
    slab_ref, col_ref, probe_ref,
    basis_ref, image_ref,
    cols, probes, yt, xall, xaug, kmat, spart, rsrecv, sfull, st,
    zacc, zsend, zmine, zcrecv, zout, zyrecv, gacc, gall, tmat, tinv,
    in_sem, sz_s, sz_r, sx_s, sx_r, rs_s, rs_r, az_s, az_r, ax_s, ax_r,
    zc_s, zc_r, zy_s, zy_r, g_s, g_r,
    *, slab_total, point_total,
):
    row = lax.axis_index("row")
    col = lax.axis_index("col")
    core = lax.rem(row, 2)
    y = lax.rem(lax.div(row, 2), 4)
    zhi = lax.div(row, 8)
    z = zhi * 4 + lax.rem(col, 4)
    x = lax.div(col, 4)
    mine = y * NCORE + core

    def at_z(r):
        return at_offset(0, r)

    def at_x(r):
        return at_offset(r, 0)

    def at_offset(dx, dz):
        gx, gz = lax.rem(x + dx, NX), lax.rem(z + dz, NZ)
        return (lax.div(gz, 4) * 8 + mine, gx * 4 + lax.rem(gz, 4))

    def at_peer(q):
        return (zhi * 8 + q, col)

    def each(lo, hi, f):
        def step(r, _):
            f(r)
            return 0

        lax.fori_loop(lo, hi, step, 0)

    def unrolled(lo, hi, f):
        for r in range(lo, hi):
            f(r)

    def remote(src, dst, send, recv, device):
        return pltpu.make_async_remote_copy(
            src_ref=src, dst_ref=dst, send_sem=send, recv_sem=recv, device_id=device, device_id_type=MESH
        )

    cp_c = pltpu.make_async_copy(col_ref.at[:, pl.ds(pl.multiple_of(zhi * B, B), B)], cols, in_sem.at[0])
    cp_p = pltpu.make_async_copy(
        probe_ref.at[:, pl.ds(pl.multiple_of(zhi * B, B), B)], probes.at[pl.ds(0, PROBES), :], in_sem.at[1]
    )
    cp_c.start()
    cp_p.start()

    barrier = pltpu.get_barrier_semaphore()

    def greet(device):
        pl.semaphore_signal(barrier, inc=1, device_id=device, device_id_type=MESH)

    for dx, dz in OTHERS:
        greet(at_offset(dx, dz))
    unrolled(1, PEERS, lambda r: greet(at_peer(lax.rem(mine + r, PEERS))))

    s_in = slab_ref[...].astype(F32)
    xall[x, z] = jnp.concatenate([s_in[: DIMS // 2], s_in[DIMS // 2 :]], axis=1).astype(BF16)
    probes[PROBES:, :] = jnp.zeros((128 - PROBES, B), BF16)

    pl.semaphore_wait(barrier, GROUP - 1 + PEERS - 1)

    def slab_z(r):
        return remote(xall.at[x, z], xall.at[x, z], sz_s.at[r - 1], sz_r.at[r - 1], at_z(r))

    def slab_x(r):
        return remote(xall.at[x], xall.at[x], sx_s.at[r - 1], sx_r.at[r - 1], at_x(r))

    for r in (4, 3, 5, 2, 6, 1, 7):
        slab_z(r).start()

    cp_c.wait()
    alpha = LOG2E * 8.0 / DIMS

    def make_yt(i):
        b0 = pl.multiple_of(i * 512, 512)
        yv = cols[:, pl.ds(b0, 512)].astype(F32)
        yp = yv * (2.0 * alpha)
        h, m, l = split3(yp)
        nh, nm, nl = split3(-alpha * jnp.sum(yv * yv, axis=0, keepdims=True))
        r = lax.broadcasted_iota(jnp.int32, (DIMS, 512), 0)
        extra = jnp.where(
            r < 3, 1.0, jnp.where(r == 3, nh, jnp.where(r == 4, nm, jnp.where(r == 5, nl, 0.0)))
        )
        yt[pl.ds(b0, 512), 0:128] = jnp.transpose(jnp.concatenate([h, m], axis=0)).astype(BF16)
        yt[pl.ds(b0, 512), 128:256] = jnp.transpose(jnp.concatenate([l, extra], axis=0)).astype(BF16)

    each(0, B // 1024, make_yt)
    unrolled(1, NZ, lambda r: slab_z(r).wait_recv())
    for r in (2, 1, 3):
        slab_x(r).start()
    each(B // 1024, B // 512, make_yt)
    cp_p.wait()

    lane = lax.broadcasted_iota(jnp.int32, (DIMS // 2, 128), 1)

    def build_x(c):
        for pair in range(NZ // 2):
            va = xall[c, 2 * pair].astype(F32)
            vb = xall[c, 2 * pair + 1].astype(F32)
            even = jnp.where(lane < 64, va, pltpu.roll(vb, 64, 1))
            odd = jnp.where(lane < 64, pltpu.roll(va, 64, 1), vb)
            xv = jnp.concatenate([even, odd], axis=0)
            nh, nm, nl = split3(-alpha * jnp.sum(xv * xv, axis=0, keepdims=True))
            r = lax.broadcasted_iota(jnp.int32, (DIMS, 128), 0)
            extra = jnp.where(
                r == 0, nh,
                jnp.where(r == 1, nm, jnp.where(r == 2, nl, jnp.where(r < 6, 1.0, 0.0))),
            )
            whole = jnp.concatenate([xv, xv, xv, extra], axis=0).astype(BF16)
            xaug[:, pair * 128 : (pair + 1) * 128] = whole

    def piece(gx, gz):
        return (
            pl.ds(pl.multiple_of(gz * 8, 8), 8), pl.ds(pl.multiple_of(gx * 128, 128), 128)
        )

    def rs(c, k):
        dx, dz = OTHERS[k]
        there = piece(lax.rem(x + dx, NX), lax.rem(z + dz, NZ))
        return remote(
            spart.at[(c, *there)], rsrecv.at[c, k], rs_s.at[c], rs_r.at[c], at_offset(dx, dz)
        )

    def to_others(f):
        for k in range(GROUP - 1):
            f(k)

    def rs_all(c):
        return remote(rsrecv.at[c], rsrecv.at[c], rs_s.at[c], rs_r.at[c], at_z(1))

    def az(c, r):
        here = sfull.at[(c, *piece(x, z))]
        return remote(here, here, az_s.at[c], az_r.at[c], at_z(r))

    def ax(c, r):
        here = sfull.at[c, :, pl.ds(pl.multiple_of(x * 128, 128), 128)]
        return remote(here, here, ax_s.at[c], ax_r.at[c], at_x(r))

    def az_all(c):
        some = rsrecv.at[c, pl.ds(0, NZ - 1)]
        return remote(some, some, az_s.at[c], az_r.at[c], at_z(1))

    def ax_all(c):
        some = rsrecv.at[c, pl.ds(0, (NX - 1) * NZ)]
        return remote(some, some, ax_s.at[c], ax_r.at[c], at_z(1))

    def sum_own(c):
        rs_all(c).wait_recv()
        sfull[(c, *piece(x, z))] = spart[(c, *piece(x, z))] + jnp.sum(rsrecv[c], axis=0)

    def reduce_own(c):
        sum_own(c)
        unrolled(1, NZ, lambda r: az(c, r).start())

    def gather_x(c):
        az_all(c).wait_recv()
        unrolled(1, NX, lambda r: ax(c, r).start())

    def chunk_at(c):
        return pl.ds(pl.multiple_of(c * CA, CA), CA)

    def tile(c, i):
        b0 = pl.multiple_of(i * TB, TB)
        t = lax.dot_general(yt[pl.ds(b0, TB), :], xaug[...], NN, preferred_element_type=F32)
        k = jnp.exp2(t).astype(BF16)
        kmat[pl.ds(b0, TB), chunk_at(c)] = k
        return lax.dot_general(probes[:, pl.ds(b0, TB)], k, NN, preferred_element_type=F32)[:PROBES]

    def clear_part(c):
        spart[c] = jnp.zeros((PROBES, CA), F32)

    each(0, CHUNKS, clear_part)

    def phase1(n):
        index = jnp.where(n == 0, 2 * x, jnp.where(n <= 2 * x, n - 1, n))
        c = index // 2
        half = index % 2

        @pl.when((half == 0) & (c != x))
        def _():
            slab_x((x - c + NX) % NX).wait_recv()

        pl.when((half == 0) | (c == x))(lambda: build_x(c))
        spart[c] += tile(c, half)
        pl.when(half == 1)(lambda: to_others(lambda k: rs(c, k).start()))
        pl.when(n == 6)(lambda: reduce_own(0))

    each(0, 2 * CHUNKS, phase1)
    reduce_own(1)
    gather_x(0)
    reduce_own(2)
    gather_x(1)

    wide = lax.broadcasted_iota(jnp.int32, (OWN // 2, 128), 1)
    glane = lax.broadcasted_iota(jnp.int32, (PROBES, 128), 1)
    grow = lax.broadcasted_iota(jnp.int32, (PROBES, 128), 0)
    gacc[...] = jnp.zeros((PROBES, 128), F32)

    def take_chunk(c):
        s = sfull[c]
        hi = s.astype(BF16).astype(F32)
        st[...] = jnp.transpose(jnp.concatenate([hi, s - hi], axis=0)).astype(BF16)

    def add_gram(c):
        s = sfull[c]
        gacc[:, 0:PROBES] += lax.dot_general(s, s, NT, precision=HIGHEST, preferred_element_type=F32)

    def g_copy(p, r):
        return remote(
            gall.at[p, mine], gall.at[p, mine], g_s.at[p * PEERS + r], g_r.at[p * PEERS + r],
            at_peer(lax.rem(mine + r, PEERS)),
        )

    def send_gram(p):
        v = gacc[...]
        gall[p, mine] = jnp.where(
            glane[:32] < 64, v[:32], pltpu.roll(v[32:], 64, 1)
        )
        unrolled(1, PEERS, lambda r: g_copy(p, r).start())

    def sum_gram(p):
        unrolled(1, PEERS, lambda r: g_copy(p, r).wait_recv())
        v = jnp.sum(gall[p], axis=0)
        both_halves = jnp.concatenate([v, pltpu.roll(v, 64, 1)], axis=0)
        return jnp.where(glane < 64, both_halves, 0.0)

    def damping():
        m = sum_gram(0)

        def trace(v):
            return jnp.sum(jnp.where(glane == grow, v, 0.0), keepdims=True)

        m = m / jnp.maximum(trace(m), 1e-30)
        for _ in range(3):
            m = lax.dot_general(m[:, :PROBES], m, NN, precision=HIGHEST, preferred_element_type=F32)
            m = m / jnp.maximum(trace(m), 1e-30)
        diag = jnp.where(glane == grow, m, 0.0)
        top = jnp.max(diag, keepdims=True)
        ucol = jnp.sum(
            jnp.where(jnp.sum(diag, axis=0, keepdims=True) == top, jnp.where(glane < 64, m, 0.0), 0.0),
            axis=1, keepdims=True,
        )
        urow = jnp.sum(
            jnp.where(jnp.sum(diag, axis=1, keepdims=True) == top, m, 0.0), axis=0, keepdims=True
        )
        uu = jnp.maximum(jnp.sum(ucol * ucol, axis=0, keepdims=True), 1e-30)
        outer = ucol * (urow + pltpu.roll(urow, 64, 1)) / uu
        eye = jnp.where((glane == grow) | (glane - 64 == grow), 1.0, 0.0)
        t = eye - 0.875 * outer
        tinv[...] = eye + 7.0 * outer
        tmat[0:PROBES, :] = jnp.where(glane < 64, t, 0.0)
        tmat[PROBES:128, :] = jnp.where(glane >= 64, t, 0.0)

    def image_part(c, t):
        yo = lax.rem(y + 1 + t, NY)
        return lax.dot_general(
            kmat[pl.ds(pl.multiple_of(yo * 2 * OWN, 2 * OWN), 2 * OWN), chunk_at(c)], st[...], NN,
            preferred_element_type=F32,
        )

    def merged(t, o):
        u = zacc[t, pl.ds(pl.multiple_of(o * OWN, OWN), OWN // 2), :]
        v = zacc[t, pl.ds(pl.multiple_of(o * OWN + OWN // 2, OWN // 2), OWN // 2), :]
        return jnp.where(wide < 64, u + pltpu.roll(u, 64, 1), v + pltpu.roll(v, 64, 1))

    def add_part(c, t):
        zacc[t] += image_part(c, t)

    def first_part(t):
        zacc[t] = image_part(0, t)

    def one_pass(c):
        ax_all(c).wait_recv()
        take_chunk(c)
        add_gram(c)
        each(0, NY, lambda t: add_part(c, t))

    reduce_own(3)
    gather_x(2)
    ax_all(0).wait_recv()
    take_chunk(0)
    add_gram(0)
    send_gram(0)
    each(0, NY, first_part)
    one_pass(1)
    gather_x(3)
    one_pass(2)
    damping()
    ax_all(CHUNKS - 1).wait_recv()
    add_gram(CHUNKS - 1)
    send_gram(1)
    take_chunk(CHUNKS - 1)

    def zc(t):
        return remote(zsend.at[t], zcrecv.at[t], zc_s.at[t], zc_r.at[t], at_peer(y * 2 + 1 - core))

    def zy(t):
        return remote(
            zout.at[t], zyrecv.at[t], zy_s.at[t], zy_r.at[t], at_peer((lax.rem(y + 1 + t, NY)) * 2 + core)
        )

    def last_part(t):
        add_part(CHUNKS - 1, t)
        zsend[t] = merged(t, 1 - core)
        zc(t).start()

    def damped(t):
        zc(t).wait_recv()
        return dot3(merged(t, core) + zcrecv[t], tmat[...], NN)

    def share(t):
        zout[t] = damped(t).astype(BF16)
        zy(t).start()

    unrolled(0, NY, last_part)
    unrolled(0, NY - 1, share)
    zmine[...] = damped(NY - 1)

    own_lanes = pl.ds(pl.multiple_of((z // 2) * 128, 128), 128)
    stile = sfull[x, :, own_lanes]
    sown = jnp.where(z % 2 == 1, pltpu.roll(stile, 64, 1), stile)
    sdamp = lax.dot_general(
        tmat[0:PROBES, 0:PROBES], sown, NN, precision=HIGHEST, preferred_element_type=F32
    )
    gram = sum_gram(1) / slab_total
    trace = jnp.sum(jnp.where(glane == grow, gram, 0.0), keepdims=True)
    m = jnp.where(glane < 64, gram, tinv[...])
    for k in range(0, PROBES, 8):
        cs, fs, rows = [], [], []
        for i in range(8):
            q = k + i
            c = jnp.broadcast_to(m[:, q : q + 1], (PROBES, 128))
            r = m[q : q + 1, :]
            for j in range(i):
                c = c - fs[j] * cs[j][q : q + 1, :]
                r = r - fs[j][q : q + 1, :] * rows[j]
            cs.append(c)
            fs.append(jnp.where(grow > q, c / c[q : q + 1, :], 0.0))
            rows.append(r)
        for f, r in zip(fs, rows):
            m = m - f * r
    d = jnp.sum(jnp.where(glane == grow, m, 0.0), axis=1, keepdims=True)
    upper = jnp.where(glane >= 64, m / jnp.sqrt(d), 0.0)
    lower = pltpu.roll(upper, 64, 1)

    basis = lax.dot_general(
        lower[:, :PROBES], sdamp, NN, precision=HIGHEST, preferred_element_type=F32
    )
    basis_ref[...] = basis[:, :BLK].astype(BF16)
    scale = jnp.sqrt(jnp.float32(PROBES * point_total) / trace) / slab_total

    each(1, NZ, lambda r: slab_z(r).wait_send())
    each(1, NX, lambda r: slab_x(r).wait_send())

    each(0, CHUNKS, lambda c: rs_all(c).wait_send())
    each(0, CHUNKS, lambda c: az_all(c).wait_send())
    each(0, CHUNKS, lambda c: ax_all(c).wait_send())
    each(0, NY, lambda t: zc(t).wait_send())
    each(0, 2, lambda p: each(1, PEERS, lambda r: g_copy(p, r).wait_send()))
    each(0, NY - 1, lambda t: zy(t).wait())
    zs = zmine[...] + (zyrecv[0].astype(F32) + zyrecv[1].astype(F32) + zyrecv[2].astype(F32))
    halves = scale * dot3(jnp.concatenate([lower, upper], axis=0), zs, NT)
    image_ref[:, : OWN // 2] = halves[:PROBES]
    image_ref[:, OWN // 2 :] = halves[PROBES:]


def finish_kernel(basis_in, image_in, basis_out, image_out):
    basis_out[...] = basis_in[...]
    image_out[...] = image_in[...]


def body(slab_points, col_points, probes):
    vmem = pl.BlockSpec(memory_space=pltpu.VMEM)
    hbm = pl.BlockSpec(memory_space=pl.ANY)
    dma = pltpu.SemaphoreType.DMA
    basis, image = pl.pallas_call(
        functools.partial(main_kernel, slab_total=A * PEERS, point_total=B * GROUP),
        out_shape=(
            jax.ShapeDtypeStruct((PROBES, BLK), BF16),
            jax.ShapeDtypeStruct((PROBES, OWN), F32),
        ),
        in_specs=[vmem, hbm, hbm],
        out_specs=(vmem, vmem),
        scratch_shapes=[
            pltpu.VMEM((DIMS, B), BF16),
            pltpu.VMEM((128, B), BF16),
            pltpu.VMEM((B, 256), BF16),
            pltpu.VMEM((NX, NZ, 32, 128), BF16),
            pltpu.VMEM((256, CA), BF16),
            pltpu.VMEM((B, A), BF16),
            pltpu.VMEM((CHUNKS, PROBES, CA), F32),
            pltpu.VMEM((CHUNKS, GROUP - 1, 8, 128), F32),
            pltpu.VMEM((CHUNKS, PROBES, CA), F32),
            pltpu.VMEM((CA, 128), BF16),
            pltpu.VMEM((NY, 2 * OWN, 128), F32),
            pltpu.VMEM((NY, OWN // 2, 128), F32),
            pltpu.VMEM((OWN // 2, 128), F32),
            pltpu.VMEM((NY, OWN // 2, 128), F32),
            pltpu.VMEM((NY - 1, OWN // 2, 128), BF16),
            pltpu.VMEM((NY - 1, OWN // 2, 128), BF16),
            pltpu.VMEM((PROBES, 128), F32),
            pltpu.VMEM((2, PEERS, 32, 128), F32),
            pltpu.VMEM((128, 128), F32),
            pltpu.VMEM((PROBES, 128), F32),
            dma((2,)),
            dma((NZ - 1,)), dma((NZ - 1,)), dma((NX - 1,)), dma((NX - 1,)),
            dma((CHUNKS,)), dma((CHUNKS,)), dma((CHUNKS,)), dma((CHUNKS,)), dma((CHUNKS,)), dma((CHUNKS,)),
            dma((NY,)), dma((NY,)), dma((NY - 1,)), dma((NY - 1,)),
            dma((2 * PEERS,)), dma((2 * PEERS,)),
        ],
        compiler_params=pltpu.CompilerParams(
            collective_id=0, has_side_effects=True, vmem_limit_bytes=62 << 20
        ),
        name="slab_kernel",
    )(slab_points, col_points, probes)
    return pl.pallas_call(
        finish_kernel,
        out_shape=(
            jax.ShapeDtypeStruct((PROBES, BLK), BF16),
            jax.ShapeDtypeStruct((PROBES, OWN), F32),
        ),
        in_specs=[vmem, vmem],
        out_specs=(vmem, vmem),
        name="finish",
    )(basis, image)


def solution(mesh):
    return jax.shard_map(
        body,
        mesh=mesh,
        in_specs=(P(None, ("row", "col")), P(None, "col"), P(None, "col")),
        out_specs=(P(None, ("row", "col")), P(None, ("col", "row"))),
        check_vma=False,
    )
```
